128 devices in a mesh: band: 4 (over z_lo, core), dom: 32 (over y, z_hi, x).
Axes of the slice: x: 4, y: 4, z: 4 (z_hi: 2, z_lo: 2; z = z_hi * 2 + z_lo), core: 2. Of those that a mesh axis runs over, the one named last changes fastest.
Arguments:
- orbitals: float32 [192, 96, 2304], P('band', 'dom'), as said below
- potential: float32 [96, 2304], P('dom'), may hold values from -1 to 1
Outputs:
- rotated: float32 [192, 96, 2304], P('band', 'dom')
The draws below stay inside these ranges and needn't reach their ends.
Inputs may be any that keep to these rules, and one draw needn't show every extreme that they name: real-valued orbitals.
All inputs are finite; a program needn't handle non-finite values.
Results may differ from the reference program's by a relative error of at most 0.00013.
Values sent between devices are 32-bit elements; how exact they have to be, the bound alone decides.
A program may use at most 192 MiB of HBM per device.

```python
import math
import jax
import jax.numpy as jnp
from jax import lax

M = 192
NY = 48
NZ = 48
PLANE = 2304
NX = 96
CELLS = 221184


def draw_orbitals(key, part):
    keys = jax.random.split(key, 3)
    shape = (M, NX, NY * NZ)
    base = jax.random.normal(keys[0], shape, jnp.float32)
    mixed = base + 0.4 * jnp.roll(base, -1, 0) - 0.3 * jnp.roll(base, -3, 0)
    column_scale = jnp.exp(jax.random.uniform(keys[1], (M, 1, 1), jnp.float32, 0.0, math.log(10.0)))
    cell_scale = jnp.exp(jax.random.uniform(keys[2], (1, NX, NY * NZ), jnp.float32, 0.0, math.log(10.0)))
    return mixed * column_scale * cell_scale


def block_levels(stream_key, extent, pieces, least, top_value):
    loudness = 1.0
    for dim, blocks in pieces:
        heights = jax.random.uniform(jax.random.fold_in(jax.random.fold_in(stream_key, 6), dim), (blocks,), jnp.float32, least / len(pieces), top_value / len(pieces))
        loudness = loudness * jnp.repeat(jnp.exp(heights), extent[dim] // blocks).reshape((-1,) + (1,) * (len(extent) - 1 - dim))
    return loudness


def setup_inputs(seed: int = 0) -> dict:
    key_list = jax.random.split(jax.random.key(seed), 3)
    return {
        "orbitals": draw_orbitals(jax.random.fold_in(key_list[2], 71), 0),
        "potential": jnp.clip(jax.random.uniform(key_list[1], (NX, PLANE), jnp.float32, -1.0, 1.0) * block_levels(key_list[1], (NX, PLANE), ((0, 32),), -0.4, 0.0), -1.0, 1.0),
    }


stencil_weights = (-5369.0 / 1800.0, 12.0 / 7.0, -15.0 / 56.0, 10.0 / 189.0, -1.0 / 112.0, 2.0 / 1925.0, -1.0 / 16632.0)
centre_shift = 7.0
half_width = 5.0

def apply_hamiltonian(padded, potential_part):
    row_count = padded.shape[0]
    inner_width = padded.shape[1] - 12
    centre = padded[:, 6:6 + inner_width]
    grid = centre.reshape(row_count, inner_width, NY, NZ)
    accumulated = 3.0 * stencil_weights[0] * centre
    for offset in range(1, 7):
        sideways = padded[:, 6 + offset:6 + offset + inner_width] + padded[:, 6 - offset:6 - offset + inner_width]
        across = jnp.roll(grid, offset, 2) + jnp.roll(grid, -offset, 2)
        across = across + jnp.roll(grid, offset, 3) + jnp.roll(grid, -offset, 3)
        sideways = sideways + across.reshape(row_count, inner_width, NY * NZ)
        accumulated = accumulated + stencil_weights[offset] * sideways
    return -0.5 * accumulated + potential_part * centre

def chebyshev_step(padded, potential_part, previous):
    centre = padded[:, 6:padded.shape[1] - 6]
    applied = apply_hamiltonian(padded, potential_part)
    if previous is None:
        return (applied - centre_shift * centre) / half_width
    return 2.0 * (applied - centre_shift * centre) / half_width - previous

def wrap_planes(field):
    return jnp.concatenate([field[:, -6:], field, field[:, :6]], axis=1)

def filter_block(orbital_block, potential):
    previous = orbital_block
    current = chebyshev_step(wrap_planes(orbital_block), potential, None)
    for step_index in range(3):
        following = chebyshev_step(wrap_planes(current), potential, previous)
        previous = current
        current = following
    return current

def reference(orbitals, potential):
    blocks = orbitals.reshape(M // 32, 32, NX, NY * NZ)
    filtered = lax.map(lambda orbital_block: filter_block(orbital_block, potential), blocks)
    filtered = filtered.reshape(M, NX * NY * NZ)
    intersection = lax.dot_general(filtered.astype(jnp.float32), filtered.astype(jnp.float32), (((1,), (1,)), ((), ())), precision=lax.Precision.HIGHEST, preferred_element_type=jnp.float32) / CELLS
    lower_factor = jnp.linalg.cholesky(intersection)
    inverse = jax.scipy.linalg.solve_triangular(lower_factor, jnp.eye(M, dtype=jnp.float32), lower=True)
    rotated = jnp.dot(inverse.astype(jnp.float32), filtered.astype(jnp.float32), precision=lax.Precision.HIGHEST, preferred_element_type=jnp.float32)
    return rotated.reshape(M, NX, NY * NZ)
```

```python
import functools

import jax
import jax.numpy as jnp
import numpy as np
from jax import lax
from jax.experimental import pallas as pl
from jax.experimental.pallas import tpu as pltpu
from jax.sharding import PartitionSpec as P

M = 192
CELLS = 221184
MESH = pl.DeviceIdType.MESH

stencil_weights = (
    -5369.0 / 1800.0,
    12.0 / 7.0,
    -15.0 / 56.0,
    10.0 / 189.0,
    -1.0 / 112.0,
    2.0 / 1925.0,
    -1.0 / 16632.0,
)
SCALE = 0.4
COEFS = [-0.5 * SCALE * w for w in stencil_weights]
DIAGONAL = 3.0 * COEFS[0] - 7.0 * SCALE
TILES = 14


def z_matrix():
    full = np.zeros((128, 128), np.float32)
    for slot in range(2):
        for z in range(48):
            for k in range(1, 7):
                full[slot * 64 + z, slot * 64 + (z + k) % 48] += COEFS[k]
                full[slot * 64 + z, slot * 64 + (z - k) % 48] += COEFS[k]
    high = full.astype(jnp.bfloat16)
    low = (full - high.astype(np.float32)).astype(jnp.bfloat16)
    row = np.concatenate([high, low], 1)
    return np.concatenate([row, row], 0)


def roll_lanes(v, by):
    by = by % 128
    return v if by == 0 else pltpu.roll(v, by, 1)


def lane_index():
    return lax.broadcasted_iota(jnp.int32, (8, 128), 1)


def unpack_y(tiles, y, shift):
    start = 48 * y
    tile, off = start // 128, start % 128
    first = roll_lanes(tiles[tile], shift - off)
    if off + 48 <= 128:
        return first
    taken = 128 - off
    second = roll_lanes(tiles[tile + 1], shift + taken)
    return jnp.where(lane_index() < shift + taken, first, second)


def pack_tile(rows, tile, shift):
    out = None
    for y in range(8):
        start = 48 * y
        lo, hi = max(start, tile * 128), min(start + 48, tile * 128 + 128)
        if lo >= hi:
            continue
        piece = roll_lanes(rows[y], start - tile * 128 - shift)
        out = piece if out is None else jnp.where(lane_index() < lo - tile * 128, out, piece)
    return out


def kernel(x_ref, p_ref, w_ref, g_ref, e_ref, recv, pot_in, field_a, field_b, pot, pack,
           part, rs_buf, xy_buf, sums, gsum, send_sems, recv_sems):
    b = lax.axis_index("band")
    d = lax.axis_index("dom")
    core = lax.rem(b, 2)
    y_pos, zh, x_pos = d // 8, lax.rem(d // 4, 2), lax.rem(d, 4)
    odd = lax.rem(d, 2)
    pair = d // 2
    two = lax.rem(core + d, 2) == 0
    first = 3 * pair + odd * (2 - core)
    me = d * 4 + b

    barrier = pltpu.get_barrier_semaphore()

    def greet(i, c):
        to = lax.rem(me + i, 128)
        pl.semaphore_signal(barrier, inc=1, device_id=(lax.rem(to, 4), to // 4), device_id_type=MESH)
        return c

    lax.fori_loop(1, 128, greet, 0)
    pl.semaphore_wait(barrier, 127)

    def piece(o):
        p = o // 3
        r = lax.rem(o, 3)
        to = 2 * p + jnp.where(r >= 2 - core, 1, 0)
        slot = jnp.where(core == 0, jnp.where(r == 1, 1, 0), jnp.where(r == 2, 1, 0))
        return to, slot

    def send_orbital(i, c):
        o = lax.rem(first + 2 + i, 48)
        to, slot = piece(o)
        src = x_ref.at[:, o, :]
        dst = recv.at[slot, lax.rem(d, 4), :, d // 4, :]

        @pl.when(to == d)
        def _():
            pltpu.make_async_copy(src, dst, recv_sems.at[slot]).start()

        @pl.when(to != d)
        def _():
            pltpu.make_async_remote_copy(
                src_ref=src, dst_ref=dst, send_sem=send_sems.at[0], recv_sem=recv_sems.at[slot],
                device_id=(b, to), device_id_type=MESH).start()
        return c

    lax.fori_loop(0, 48, send_orbital, 0)
    pot_dst = pot_in.at[lax.rem(d, 4), :, d // 4, :]
    pltpu.make_async_copy(p_ref, pot_dst, recv_sems.at[2]).start()

    def send_potential(i, c):
        to = lax.rem(d + i, 32)
        pltpu.make_async_remote_copy(
            src_ref=p_ref, dst_ref=pot_dst, send_sem=send_sems.at[1], recv_sem=recv_sems.at[2],
            device_id=(b, to), device_id_type=MESH).start()
        return c

    lax.fori_loop(1, 32, send_potential, 0)

    pltpu.make_async_copy(recv.at[0], recv.at[0], recv_sems.at[0]).wait()

    @pl.when(two)
    def _():
        pltpu.make_async_copy(recv.at[1], recv.at[1], recv_sems.at[1]).wait()

    @pl.when(jnp.logical_not(two))
    def _():
        recv[1] = jnp.zeros_like(recv[1])

    pltpu.make_async_copy(pot_in, pot_in, recv_sems.at[2]).wait()

    def unpack(n, c):
        yb = n // 12
        xi = lax.rem(n, 12)
        q, j = xi // 3, lax.rem(xi, 3)
        lanes = [pl.ds(pl.multiple_of(yb * 384 + 128 * t, 128), 128) for t in range(3)]
        left = [recv[0, q, j, :, s] for s in lanes]
        right = [recv[1, q, j, :, s] for s in lanes]
        potential = [pot_in[q, j, :, s] for s in lanes]
        lane = lane_index()
        rows = pl.ds(pl.multiple_of(xi * 8, 8), 8)
        for y in range(8):
            both = jnp.where(lane < 64, unpack_y(left, y, 0), unpack_y(right, y, 64))
            field_a[yb * 8 + y, rows, :] = both
            v = jnp.where(lane < 64, unpack_y(potential, y, 0), unpack_y(potential, y, 64))
            pot[yb * 8 + y, rows, :] = v * SCALE + DIAGONAL
        return c

    lax.fori_loop(0, 72, unpack, 0)

    def step(src, dst, is_first):
        def row(y, c):
            own = src[y]
            high = own.astype(jnp.bfloat16)
            low = (own - high.astype(jnp.float32)).astype(jnp.bfloat16)
            along_z = jnp.dot(jnp.concatenate([high, low], 1), w_ref[...],
                              preferred_element_type=jnp.float32)
            regs = [own[8 * i:8 * i + 8] for i in range(12)]
            before = {i: pltpu.roll(regs[i], 1, 0) for i in range(6, 12)}
            after = {i: pltpu.roll(regs[i], 7, 0) for i in range(6)}
            at = lambda i: before[i + 12] if i < 0 else (after[i - 12] if i >= 12 else regs[i])
            up = [lax.rem(y + k, 48) for k in range(1, 7)]
            down = [lax.rem(y + 48 - k, 48) for k in range(1, 7)]
            for i in range(12):
                rows = pl.ds(8 * i, 8)
                acc = regs[i] * pot[y, rows, :]
                acc = acc + (along_z[8 * i:8 * i + 8, :128] + along_z[8 * i:8 * i + 8, 128:])
                for k in range(1, 7):
                    near = (at(i + k) + at(i - k)) + (src[up[k - 1], rows, :] + src[down[k - 1], rows, :])
                    acc = acc + COEFS[k] * near
                dst[y, rows, :] = 0.5 * acc if is_first else acc - dst[y, rows, :]
            return c

        lax.fori_loop(0, 48, row, 0)

    step(field_a, field_b, True)
    step(field_b, field_a, False)
    step(field_a, field_b, False)
    step(field_b, field_a, False)

    def repack(n, c):
        yb = n // 12
        xi = lax.rem(n, 12)
        q, j = xi // 3, lax.rem(xi, 3)
        rows = [field_a[yb * 8 + y, pl.ds(pl.multiple_of(xi * 8, 8), 8), :] for y in range(8)]
        for t in range(3):
            for slot in range(2):
                pack[q, j * 18 + yb * 3 + t, slot] = pack_tile(rows, t, 64 * slot)
        return c

    lax.fori_loop(0, 72, repack, 0)

    def spread(count):
        def send(i, c):
            to = lax.rem(me + i, 128)
            to_b, to_d = lax.rem(to, 4), to // 4
            begin = 14 * to_b - jnp.maximum(to_b - 1, 0)
            src = pack.at[lax.rem(to_d, 4), pl.ds(begin, TILES), pl.ds(0, count), to_d // 4, :]
            dst = e_ref.at[to_b, :, pl.ds(48 * b + first, count), :]
            pltpu.make_async_remote_copy(
                src_ref=src, dst_ref=dst, send_sem=send_sems.at[2], recv_sem=recv_sems.at[3],
                device_id=(to_b, to_d), device_id_type=MESH).start()
            return c

        lax.fori_loop(1, 128, send, 0)
        begin = 14 * b - jnp.maximum(b - 1, 0)
        pltpu.make_async_copy(
            pack.at[lax.rem(d, 4), pl.ds(begin, TILES), pl.ds(0, count), d // 4, :],
            e_ref.at[b, :, pl.ds(48 * b + first, count), :], recv_sems.at[3]).start()

    @pl.when(two)
    def _():
        spread(2)

    @pl.when(jnp.logical_not(two))
    def _():
        spread(1)

    pltpu.make_async_copy(e_ref.at[b], e_ref.at[b], recv_sems.at[3]).wait()

    for i in range(1, 4):
        to = lax.rem(b + i, 4)
        pltpu.make_async_remote_copy(
            src_ref=e_ref.at[b], dst_ref=e_ref.at[b], send_sem=send_sems.at[3],
            recv_sem=recv_sems.at[7 + i], device_id=(to, d), device_id_type=MESH).start()

    def gram(left, right):
        return lax.dot_general(left, right, (((1,), (1,)), ((), ())), precision=lax.Precision.HIGHEST,
                               preferred_element_type=jnp.float32)

    total = jnp.zeros((M, M), jnp.float32)
    for i in range(0, TILES, 2):
        one = e_ref[b, i]
        if i == 0:
            one = jnp.where(b >= 2, 0.0, one)
        both = jnp.concatenate([one, e_ref[b, i + 1]], 1)
        total = total + gram(both, both)
    part[:, :, 0:128] = total[:, :128].reshape(8, 24, 128)
    part[:, :, 128:256] = jnp.concatenate([total[:, 128:], jnp.zeros((M, 64), jnp.float32)], 1).reshape(8, 24, 128)

    mine = zh * 4 + b
    rs_buf[mine] = part[mine]
    for i in range(1, 8):
        to = lax.rem(mine + i, 8)
        pltpu.make_async_remote_copy(
            src_ref=part.at[to], dst_ref=rs_buf.at[mine], send_sem=send_sems.at[4], recv_sem=recv_sems.at[4],
            device_id=(lax.rem(to, 4), y_pos * 8 + (to // 4) * 4 + x_pos), device_id_type=MESH).start()
    pltpu.make_async_copy(rs_buf.at[pl.ds(0, 7)], rs_buf.at[pl.ds(0, 7)], recv_sems.at[4]).wait()
    acc = rs_buf[0]
    for i in range(1, 8):
        acc = acc + rs_buf[i]
    sums[...] = acc
    spot = y_pos * 4 + x_pos
    xy_buf[spot] = acc
    for i in range(1, 16):
        to = lax.rem(spot + i, 16)
        pltpu.make_async_remote_copy(
            src_ref=sums, dst_ref=xy_buf.at[spot], send_sem=send_sems.at[5], recv_sem=recv_sems.at[5],
            device_id=(b, (to // 4) * 8 + zh * 4 + lax.rem(to, 4)), device_id_type=MESH).start()
    pltpu.make_async_copy(xy_buf.at[pl.ds(0, 15)], xy_buf.at[pl.ds(0, 15)], recv_sems.at[5]).wait()
    acc = xy_buf[0]
    for i in range(1, 16):
        acc = acc + xy_buf[i]
    gsum[...] = acc
    g_ref[mine] = acc
    for i in range(1, 8):
        to = lax.rem(mine + i, 8)
        pltpu.make_async_remote_copy(
            src_ref=gsum, dst_ref=g_ref.at[mine], send_sem=send_sems.at[6], recv_sem=recv_sems.at[6],
            device_id=(lax.rem(to, 4), y_pos * 8 + (to // 4) * 4 + x_pos), device_id_type=MESH).start()
    pltpu.make_async_copy(g_ref.at[pl.ds(0, 7)], g_ref.at[pl.ds(0, 7)], recv_sems.at[6]).wait()

    for i in range(1, 4):
        pltpu.make_async_copy(e_ref.at[b], e_ref.at[b], recv_sems.at[7 + i]).wait()

    def drain(ref, sem, times):
        def body(i, c):
            pltpu.make_async_copy(ref, ref, sem).wait()
            return c
        lax.fori_loop(0, times, body, 0)

    orbital = recv.at[0, 0, :, 0, :]
    drain(orbital, send_sems.at[0], jnp.where(two, 46, 47))
    drain(orbital, send_sems.at[1], 31)
    share = pack.at[0, pl.ds(0, TILES), pl.ds(0, 1), 0, :]
    drain(share, send_sems.at[2], jnp.where(two, 254, 127))
    drain(e_ref.at[0], send_sems.at[3], 3)
    drain(part.at[0], send_sems.at[4], 7)
    drain(sums, send_sems.at[5], 15)
    drain(sums, send_sems.at[6], 7)


def per_device(orbitals, potential):
    f32 = jnp.float32
    vmem = pl.BlockSpec(memory_space=pltpu.VMEM)
    g, e = pl.pallas_call(
        kernel,
        out_shape=(jax.ShapeDtypeStruct((8, 24, 256), f32),
                   jax.ShapeDtypeStruct((4, TILES, M, 128), f32)),
        in_specs=[pl.BlockSpec(memory_space=pl.ANY), vmem, vmem],
        out_specs=(vmem, vmem),
        scratch_shapes=[
            pltpu.VMEM((2, 4, 3, 8, 2304), f32),
            pltpu.VMEM((4, 3, 8, 2304), f32),
            pltpu.VMEM((48, 96, 128), f32),
            pltpu.VMEM((48, 96, 128), f32),
            pltpu.VMEM((48, 96, 128), f32),
            pltpu.VMEM((4, 54, 2, 8, 128), f32),
            pltpu.VMEM((8, 24, 256), f32),
            pltpu.VMEM((8, 24, 256), f32),
            pltpu.VMEM((16, 24, 256), f32),
            pltpu.VMEM((24, 256), f32),
            pltpu.VMEM((24, 256), f32),
            pltpu.SemaphoreType.DMA((7,)),
            pltpu.SemaphoreType.DMA((11,)),
        ],
        compiler_params=pltpu.CompilerParams(
            collective_id=0, has_side_effects=True, vmem_limit_bytes=48 * 2**20),
    )(jnp.transpose(orbitals, (1, 0, 2)), potential, jnp.asarray(z_matrix()))
    intersection = g.reshape(M, 256)[:, :M] / CELLS
    lower = jnp.linalg.cholesky(intersection)
    inverse = jax.scipy.linalg.solve_triangular(lower, jnp.eye(M, dtype=f32), lower=True)
    own = lax.dynamic_slice_in_dim(inverse, lax.axis_index("band") * 48, 48, 0)
    everyone = jnp.concatenate([e[0], e[1], e[2, 1:], e[3, 1:]], 0)
    out = jnp.einsum("ij,tjc->tic", own, everyone, precision=lax.Precision.HIGHEST,
                     preferred_element_type=f32)
    return out.reshape(3, 18, 48, 128).transpose(2, 0, 1, 3).reshape(48, 3, 2304)


def solution(mesh):
    placed = (P("band", "dom", None), P("dom", None))
    return jax.shard_map(
        per_device, mesh=mesh, in_specs=placed, out_specs=P("band", "dom", None), check_vma=False
    )
```

```python
import jax
import jax.numpy as jnp
import numpy as np
from jax import lax
from jax.experimental import pallas as pl
from jax.experimental.pallas import tpu as pltpu
from jax.sharding import PartitionSpec as P

M = 192
CELLS = 221184
MESH = pl.DeviceIdType.MESH
F32, BF16 = jnp.float32, jnp.bfloat16

stencil_weights = (
    -5369.0 / 1800.0,
    12.0 / 7.0,
    -15.0 / 56.0,
    10.0 / 189.0,
    -1.0 / 112.0,
    2.0 / 1925.0,
    -1.0 / 16632.0,
)
SCALE = 0.4
COEFS = [-0.5 * SCALE * w for w in stencil_weights]
DIAGONAL = 3.0 * COEFS[0] - 7.0 * SCALE
TILES = 14
ROWS = 8


def two_terms(full):
    high = full.astype(BF16)
    return high, (full - high.astype(np.float32)).astype(BF16)


def z_matrix():
    full = np.zeros((128, 128), np.float32)
    for slot in range(2):
        for z in range(48):
            for k in range(1, 7):
                full[slot * 64 + z, slot * 64 + (z + k) % 48] += COEFS[k]
                full[slot * 64 + z, slot * 64 + (z - k) % 48] += COEFS[k]
    row = np.concatenate(two_terms(full), 1)
    return np.concatenate([row, row], 0)


def x_matrix():
    full = np.zeros((96, 96), np.float32)
    place = [(r % 8) * 12 + r // 8 for r in range(96)]
    for a in range(96):
        for c in range(96):
            away = (place[a] - place[c]) % 96
            away = min(away, 96 - away)
            if 1 <= away <= 6:
                full[a, c] = COEFS[away]
    high, low = two_terms(full)
    return np.concatenate([np.concatenate([high, high], 1), np.concatenate([low, low], 1)], 0)


def roll_lanes(v, by):
    by = by % 128
    return v if by == 0 else pltpu.roll(v, by, 1)


def lane_index():
    return lax.broadcasted_iota(jnp.int32, (8, 128), 1)


def to_rows(left, right):
    lane = lane_index()
    turned = [roll_lanes(v, 64) for v in right]
    rows = []
    for y in range(8):
        tile, off = 48 * y // 128, 48 * y % 128
        if off + 48 <= 128:
            inside = jnp.logical_and(lane >= off, lane < off + 48)
            mixed = jnp.where(inside, left[tile], turned[tile])
        else:
            mixed = jnp.where(lane < 64, turned[tile], turned[tile + 1])
            mixed = jnp.where(lane < off - 80, left[tile + 1], mixed)
            mixed = jnp.where(lane >= off, left[tile], mixed)
        rows.append(roll_lanes(mixed, -off))
    return rows


def to_tiles(rows):
    lane = lane_index()
    turned_lane = lax.rem(lane + 64, 128)
    placed = [roll_lanes(rows[y], 48 * y % 128) for y in range(8)]
    left, right = [], []
    for tile in range(3):
        a = c = None
        for y in range(8):
            lo, hi = max(48 * y, tile * 128), min(48 * y + 48, tile * 128 + 128)
            if lo >= hi:
                continue
            if a is None:
                a = c = placed[y]
            else:
                a = jnp.where(lane < lo - tile * 128, a, placed[y])
                c = jnp.where(turned_lane < lo - tile * 128, c, placed[y])
        left.append(a)
        right.append(roll_lanes(c, 64))
    return left, right


def three_terms(v):
    parts = []
    for _ in range(3):
        part = v.astype(BF16).astype(F32)
        parts.append(part)
        v = v - part
    return parts


def invert_factor(r, out):
    lane = lax.broadcasted_iota(jnp.int32, (8, 128), 1)
    sub = lax.broadcasted_iota(jnp.int32, (8, 128), 0)
    splat = lambda v, i, j: jnp.broadcast_to(v[i:i + 1, j:j + 1], (8, 128))
    spread = lambda v, i: jnp.broadcast_to(v[i:i + 1], (8, 128))

    def body(first_row, k):
        rows = pl.ds(pl.multiple_of(8 * k, 8), 8)
        top = [r[rows, 0:128], r[rows, 128:256]]
        off = 8 * lax.rem(k, 16)
        block = pltpu.roll(jnp.where(k >= 16, top[1], top[0]), lax.rem(128 - off, 128), 1)
        s = {(i, j): splat(block, j, i) for i in range(8) for j in range(i + 1)}
        recip, low = [], {}
        for col in range(8):
            recip.append(1.0 / s[col, col])
            for i in range(col + 1, 8):
                low[i, col] = s[i, col] * recip[col]
            for i in range(col + 1, 8):
                for j in range(col + 1, i + 1):
                    s[i, j] = s[i, j] - low[i, col] * s[j, col]
        inv = {}
        for j in range(8):
            for i in range(j + 1, 8):
                t = low[i, j]
                for p in range(j + 1, i):
                    t = t + low[i, p] * inv[p, j]
                inv[i, j] = -t
        cols, cols_t = [], []
        for j in range(8):
            v = jnp.where(sub == j, 1.0, 0.0)
            for i in range(j + 1, 8):
                v = jnp.where(sub == i, inv[i, j], v)
            cols.append(v)
            w = jnp.where(sub == j, 1.0, 0.0)
            for i in range(j):
                w = jnp.where(sub == i, inv[j, i], w)
            cols_t.append(w)
        pivot = recip[0]
        for i in range(1, 8):
            pivot = jnp.where(sub == i, recip[i], pivot)
        zs, ss = [], []
        for t in range(2):
            local = lane + 128 * t - 8 * k
            inside = jnp.logical_and(local >= 0, local < 8)
            v = jnp.where(inside, jnp.where(local == sub, 1.0, 0.0), top[t])
            y = cols[0] * spread(v, 0)
            for j in range(1, 8):
                y = y + cols[j] * spread(v, j)
            out[rows, 128 * t:128 * t + 128] = jnp.where(local < 8, y * jnp.sqrt(pivot), 0.0)
            y = y * pivot
            z = cols_t[0] * spread(y, 0)
            for j in range(1, 8):
                z = z + cols_t[j] * spread(y, j)
            zs.append(z)
            ss.append(jnp.where(local < 8, 0.0, top[t]))
        z, w = three_terms(jnp.concatenate(zs, 1)), three_terms(jnp.concatenate(ss, 1))
        left = jnp.concatenate([w[0], w[0], w[1], w[0], w[1], w[2]], 0).astype(BF16)
        right = jnp.concatenate([z[0], z[1], z[0], z[2], z[1], z[0]], 0).astype(BF16)
        live = slice(8 * first_row, M)
        update = lax.dot_general(left[:, live], right, (((0,), (0,)), ((), ())),
                                 preferred_element_type=F32)
        local = lax.broadcasted_iota(jnp.int32, (M - 8 * first_row, 256), 1) - 8 * k
        inside = jnp.logical_and(local >= 0, local < 8)
        r[live, :] = jnp.where(inside, 0.0, r[live, :]) - update

    for part in range(3):
        def segment(k, c):
            body(8 * part, k)
            return c
        lax.fori_loop(8 * part, 8 * part + 8, segment, 0)


def kernel(x_ref, p_ref, w_hbm, c_hbm, out_ref, recv, pot_in, w_ref, c_ref, field_a, field_b, pot, pack,
           own, part, rs_buf, xy_buf, sums, gsum, packed, work, inv_ref, rot, send_sems, recv_sems):
    b = lax.axis_index("band")
    d = lax.axis_index("dom")
    core = lax.rem(b, 2)
    y_pos, zh, x_pos = d // 8, lax.rem(d // 4, 2), lax.rem(d, 4)
    two = lax.rem(core + d, 2) == 0
    first = 3 * (d // 2) + lax.rem(d, 2) * (2 - core)
    me = d * 4 + b
    partner = b + 1 - 2 * core

    def remote(src, dst, send, receive, to_b, to_d):
        pltpu.make_async_remote_copy(
            src_ref=src, dst_ref=dst, send_sem=send_sems.at[send], recv_sem=recv_sems.at[receive],
            device_id=(to_b, to_d), device_id_type=MESH).start()

    def local(src, dst, receive):
        pltpu.make_async_copy(src, dst, recv_sems.at[receive]).start()

    def arrived(ref, receive):
        pltpu.make_async_copy(ref, ref, recv_sems.at[receive]).wait()

    barrier = pltpu.get_barrier_semaphore()

    def greet(i, c):
        to = lax.rem(me + i, 128)
        pl.semaphore_signal(barrier, inc=1, device_id=(lax.rem(to, 4), to // 4), device_id_type=MESH)
        return c

    lax.fori_loop(1, 128, greet, 0)
    pl.semaphore_wait(barrier, 127)

    def send_orbital(i, c):
        o = lax.rem(first + 2 + i, 48)
        r = lax.rem(o, 3)
        to = 2 * (o // 3) + jnp.where(r >= 2 - core, 1, 0)
        slot = jnp.where(r == 1 + core, 1, 0)
        src = x_ref.at[:, o, :]
        dst = recv.at[slot, lax.rem(d, 4), :, d // 4, :]

        @pl.when(to == d)
        def _():
            local(src, dst, slot)

        @pl.when(to != d)
        def _():
            remote(src, dst, 0, slot, b, to)
        return c

    lax.fori_loop(0, 48, send_orbital, 0)
    half = p_ref.at[:, pl.ds(pl.multiple_of(1152 * core, 128), 1152)]
    half_dst = pot_in.at[core, lax.rem(d, 4), :, d // 4, :]
    local(half, half_dst, 2)

    def send_potential(i, c):
        remote(half, half_dst, 1, 2, b, lax.rem(d + i, 32))
        return c

    lax.fori_loop(1, 32, send_potential, 0)
    local(w_hbm, w_ref, 12)
    local(c_hbm, c_ref, 13)

    @pl.when(jnp.logical_not(two))
    def _():
        recv[1] = jnp.zeros_like(recv[1])

    arrived(recv.at[0], 0)

    @pl.when(two)
    def _():
        arrived(recv.at[1], 1)

    arrived(w_ref, 12)
    arrived(c_ref, 13)

    def unpack(n, c):
        yb, q = n // 4, lax.rem(n, 4)
        lanes = [pl.ds(pl.multiple_of(yb * 384 + 128 * t, 128), 128) for t in range(3)]
        for j in range(3):
            rows = to_rows([recv[0, q, j, :, s] for s in lanes], [recv[1, q, j, :, s] for s in lanes])
            for y in range(8):
                field_a[yb * 8 + y, pl.ds(pl.multiple_of(q * 24 + 8 * j, 8), 8), :] = rows[y]
        return c

    lax.fori_loop(0, 24, unpack, 0)

    def step(src, dst, begin, end, is_first):
        def block(n, c):
            y0 = n * ROWS
            values = src[pl.ds(y0, ROWS)].reshape(ROWS * 96, 128)
            high = values.astype(BF16)
            low = (values - high.astype(F32)).astype(BF16)
            along_z = jnp.dot(jnp.concatenate([high, low], 1), w_ref[...], preferred_element_type=F32)
            along_x = []
            for r in range(0, ROWS, 2):
                one, other = slice(96 * r, 96 * r + 96), slice(96 * r + 96, 96 * r + 192)
                columns = jnp.concatenate([jnp.concatenate([high[one], high[other]], 1),
                                           jnp.concatenate([low[one], low[other]], 1)], 0)
                along_x.append(jnp.dot(c_ref[...], columns, preferred_element_type=F32))
            at = [lax.rem(y0 + 48 + s, 48) for s in range(-6, ROWS + 6)]
            for r in range(ROWS):
                for i in range(12):
                    rows = pl.ds(8 * i, 8)
                    centre = src[y0 + r, rows, :]
                    acc = centre * (DIAGONAL if is_first else pot[y0 + r, rows, :])
                    for k in range(1, 7):
                        acc = acc + COEFS[k] * (src[at[6 + r + k], rows, :] + src[at[6 + r - k], rows, :])
                    z = along_z[96 * r + 8 * i:96 * r + 8 * i + 8]
                    half_lanes = slice(128 * (r % 2), 128 * (r % 2) + 128)
                    x = (along_x[r // 2][8 * i:8 * i + 8, half_lanes]
                         + along_x[r // 2][96 + 8 * i:96 + 8 * i + 8, half_lanes])
                    acc = acc + ((z[:, :128] + z[:, 128:]) + x)
                    dst[y0 + r, rows, :] = 0.5 * acc if is_first else acc - dst[y0 + r, rows, :]
            return c

        lax.fori_loop(begin, end, block, 0)

    step(field_a, field_b, 0, 4, True)
    arrived(pot_in.at[core], 2)
    remote(pot_in.at[core], pot_in.at[core], 7, 11, partner, d)
    step(field_a, field_b, 4, 6, True)
    arrived(pot_in.at[core], 11)

    def unpack_potential(n, c):
        yb, q = n // 4, lax.rem(n, 4)
        lanes = [pl.ds(pl.multiple_of(lax.rem(yb, 3) * 384 + 128 * t, 128), 128) for t in range(3)]
        for j in range(3):
            planes = [pot_in[yb // 3, q, j, :, s] for s in lanes]
            rows = to_rows(planes, planes)
            for y in range(8):
                here = pl.ds(pl.multiple_of(q * 24 + 8 * j, 8), 8)
                v = SCALE * rows[y]
                pot[yb * 8 + y, here, :] = v + DIAGONAL
                field_b[yb * 8 + y, here, :] = field_b[yb * 8 + y, here, :] + (0.5 * v) * field_a[yb * 8 + y, here, :]
        return c

    lax.fori_loop(0, 24, unpack_potential, 0)
    step(field_b, field_a, 0, 6, False)
    step(field_a, field_b, 0, 6, False)
    step(field_b, field_a, 0, 6, False)

    def repack(n, c):
        yb, q = n // 4, lax.rem(n, 4)
        for j in range(3):
            rows = [field_a[yb * 8 + y, pl.ds(pl.multiple_of(q * 24 + 8 * j, 8), 8), :] for y in range(8)]
            left, right = to_tiles(rows)
            for t in range(3):
                pack[q, j * 18 + yb * 3 + t, 0] = left[t]
                pack[q, j * 18 + yb * 3 + t, 1] = right[t]
        return c

    lax.fori_loop(0, 24, repack, 0)

    def quarter(band):
        return 14 * band - jnp.maximum(band - 1, 0)

    def spread(count):
        def send(i, c):
            to = lax.rem(me + i, 128)
            to_b, to_d = lax.rem(to, 4), to // 4
            src = pack.at[lax.rem(to_d, 4), pl.ds(quarter(to_b), TILES), pl.ds(0, count), to_d // 4, :]
            remote(src, own.at[:, pl.ds(48 * b + first, count), :], 2, 3, to_b, to_d)
            return c

        lax.fori_loop(1, 128, send, 0)
        local(pack.at[lax.rem(d, 4), pl.ds(quarter(b), TILES), pl.ds(0, count), d // 4, :],
              own.at[:, pl.ds(48 * b + first, count), :], 3)

    @pl.when(two)
    def _():
        spread(2)

    @pl.when(jnp.logical_not(two))
    def _():
        spread(1)

    arrived(own, 3)

    total = jnp.zeros((M, M), F32)
    for i in range(0, TILES, 2):
        one = own[i]
        if i == 0:
            one = jnp.where(b >= 2, 0.0, one)
        both = jnp.concatenate([one, own[i + 1]], 1)
        total = total + lax.dot_general(both, both, (((1,), (1,)), ((), ())), precision=lax.Precision.HIGHEST,
                                        preferred_element_type=F32)
    near = total[:, :128]
    far = jnp.concatenate([total[:, 128:], jnp.zeros((M, 64), F32)], 1)
    left_half = lax.broadcasted_iota(jnp.int32, (64, 128), 1) < 64
    packed[0:64] = near[0:64]
    packed[64:128] = jnp.where(left_half, far[0:64], near[64:128])
    packed[128:192] = jnp.where(left_half, far[64:128], pltpu.roll(far[128:192], 64, 1))
    for i in range(8):
        part[i] = packed[24 * i:24 * i + 24]

    mine = zh * 4 + b
    for i in range(1, 8):
        to = lax.rem(mine + i, 8)
        remote(part.at[to], rs_buf.at[mine], 4, 4, lax.rem(to, 4), y_pos * 8 + (to // 4) * 4 + x_pos)
    rs_buf[mine] = part[mine]
    arrived(rs_buf.at[pl.ds(0, 7)], 4)
    acc = rs_buf[0]
    for i in range(1, 8):
        acc = acc + rs_buf[i]
    sums[...] = acc
    spot = y_pos * 4 + x_pos
    for i in range(1, 16):
        to = lax.rem(spot + i, 16)
        remote(sums, xy_buf.at[spot], 5, 5, b, (to // 4) * 8 + zh * 4 + lax.rem(to, 4))
    xy_buf[spot] = acc
    arrived(xy_buf.at[pl.ds(0, 15)], 5)
    acc = xy_buf[0]
    for i in range(1, 16):
        acc = acc + xy_buf[i]
    acc = acc / CELLS
    gsum[mine] = acc
    for i in range(1, 8):
        to = lax.rem(mine + i, 8)
        remote(gsum.at[mine], gsum.at[mine], 6, 6, lax.rem(to, 4), y_pos * 8 + (to // 4) * 4 + x_pos)
    arrived(gsum.at[pl.ds(0, 7)], 6)

    for i in range(8):
        packed[24 * i:24 * i + 24] = gsum[i]
    work[0:64, 0:128] = packed[0:64]
    work[0:64, 128:256] = packed[64:128]
    work[64:128, 0:128] = packed[64:128]
    work[64:128, 128:256] = packed[128:192]
    work[128:192, 0:128] = packed[128:192]
    work[128:192, 128:256] = pltpu.roll(packed[128:192], 64, 1)
    invert_factor(work, inv_ref)

    def rotate(n, c):
        columns = jnp.concatenate([own[2 * n], own[2 * n + 1]], 1)
        product = jnp.dot(inv_ref[:, 0:M], columns, precision=lax.Precision.HIGHEST, preferred_element_type=F32)
        for i in range(2):
            tile = quarter(b) + 2 * n + i
            place = out_ref.at[tile // 18, :, pl.ds(pl.multiple_of(128 * lax.rem(tile, 18), 128), 128)]
            for band in range(4):
                rot[2 * n + i, band] = product[48 * band:48 * band + 48, 128 * i:128 * i + 128]

            @pl.when(jnp.logical_or(b < 2, 2 * n + i > 0))
            def _():
                for away in (2, 3, 1):
                    to = lax.rem(b + away, 4)
                    remote(rot.at[2 * n + i, to], place, 8, 7 + b, to, d)
                local(rot.at[2 * n + i, b], place, 7 + b)
        return c

    lax.fori_loop(0, TILES // 2, rotate, 0)

    def drain(ref, sem, times):
        def body(i, c):
            pltpu.make_async_copy(ref, ref, sem).wait()
            return c
        lax.fori_loop(0, times, body, 0)

    tile = rot.at[0, 0]
    mine_tiles = jnp.where(b < 2, 14, 13)
    for band in range(4):
        arrived(rot.at[pl.ds(0, 14 if band < 2 else 13), 0], 7 + band)
    drain(tile, send_sems.at[8], 3 * mine_tiles)
    orbital = recv.at[0, 0, :, 0, :]
    drain(orbital, send_sems.at[0], jnp.where(two, 46, 47))
    drain(half_dst, send_sems.at[1], 31)
    drain(pot_in.at[0], send_sems.at[7], 1)
    share = pack.at[0, pl.ds(0, TILES), pl.ds(0, 1), 0, :]
    drain(share, send_sems.at[2], jnp.where(two, 254, 127))
    drain(sums, send_sems.at[4], 7)
    drain(sums, send_sems.at[5], 15)
    drain(sums, send_sems.at[6], 7)


def per_device(orbitals, potential):
    anywhere = pl.BlockSpec(memory_space=pl.ANY)
    out = pl.pallas_call(
        kernel,
        out_shape=jax.ShapeDtypeStruct((3, 48, 2304), F32),
        in_specs=[anywhere] * 4,
        out_specs=pl.BlockSpec(memory_space=pltpu.VMEM),
        scratch_shapes=[
            pltpu.VMEM((2, 4, 3, 8, 2304), F32),
            pltpu.VMEM((2, 4, 3, 8, 1152), F32),
            pltpu.VMEM((256, 256), BF16),
            pltpu.VMEM((192, 192), BF16),
            pltpu.VMEM((48, 96, 128), F32),
            pltpu.VMEM((48, 96, 128), F32),
            pltpu.VMEM((48, 96, 128), F32),
            pltpu.VMEM((4, 54, 2, 8, 128), F32),
            pltpu.VMEM((TILES, M, 128), F32),
            pltpu.VMEM((8, 24, 128), F32),
            pltpu.VMEM((8, 24, 128), F32),
            pltpu.VMEM((16, 24, 128), F32),
            pltpu.VMEM((24, 128), F32),
            pltpu.VMEM((8, 24, 128), F32),
            pltpu.VMEM((M, 128), F32),
            pltpu.VMEM((M, 256), F32),
            pltpu.VMEM((M, 256), F32),
            pltpu.VMEM((TILES, 4, 48, 128), F32),
            pltpu.SemaphoreType.DMA((9,)),
            pltpu.SemaphoreType.DMA((14,)),
        ],
        compiler_params=pltpu.CompilerParams(
            collective_id=0, has_side_effects=True, vmem_limit_bytes=56 * 2**20),
    )(jnp.transpose(orbitals, (1, 0, 2)), potential, jnp.asarray(z_matrix()), jnp.asarray(x_matrix()))
    return jnp.transpose(out, (1, 0, 2))


def solution(mesh):
    placed = (P("band", "dom", None), P("dom", None))
    return jax.shard_map(
        per_device, mesh=mesh, in_specs=placed, out_specs=P("band", "dom", None), check_vma=False
    )
```

```python
import jax
import jax.numpy as jnp
import numpy as np
from jax import lax
from jax.experimental import pallas as pl
from jax.experimental.pallas import tpu as pltpu
from jax.sharding import PartitionSpec as P

M = 192
CELLS = 221184
MESH = pl.DeviceIdType.MESH
F32, BF16 = jnp.float32, jnp.bfloat16

stencil_weights = (
    -5369.0 / 1800.0,
    12.0 / 7.0,
    -15.0 / 56.0,
    10.0 / 189.0,
    -1.0 / 112.0,
    2.0 / 1925.0,
    -1.0 / 16632.0,
)
SCALE = 0.4
COEFS = [-0.5 * SCALE * w for w in stencil_weights]
DIAGONAL = 3.0 * COEFS[0] - 7.0 * SCALE
TILES = 14
ROWS = 8


def two_terms(full):
    high = full.astype(BF16)
    return high, (full - high.astype(np.float32)).astype(BF16)


def z_matrix():
    full = np.zeros((128, 128), np.float32)
    for half in range(2):
        for z in range(48):
            for k in range(1, 7):
                full[half * 64 + z, half * 64 + (z + k) % 48] += COEFS[k]
                full[half * 64 + z, half * 64 + (z - k) % 48] += COEFS[k]
    row = np.concatenate(two_terms(full), 1)
    return np.concatenate([row, row], 0)


def x_matrix():
    full = np.zeros((96, 96), np.float32)
    place = [(r % 8) * 12 + r // 8 for r in range(96)]
    for a in range(96):
        for c in range(96):
            away = (place[a] - place[c]) % 96
            away = min(away, 96 - away)
            if 1 <= away <= 6:
                full[a, c] = COEFS[away]
    high, low = two_terms(full)
    return np.concatenate([np.concatenate([high, high], 1), np.concatenate([low, low], 1)], 0)


def roll_lanes(v, by):
    by = by % 128
    return v if by == 0 else pltpu.roll(v, by, 1)


def lane_index():
    return lax.broadcasted_iota(jnp.int32, (8, 128), 1)


def to_rows(left, right):
    lane = lane_index()
    turned = [roll_lanes(v, 64) for v in right]
    rows = []
    for y in range(8):
        tile, off = 48 * y // 128, 48 * y % 128
        if off + 48 <= 128:
            inside = jnp.logical_and(lane >= off, lane < off + 48)
            mixed = jnp.where(inside, left[tile], turned[tile])
        else:
            mixed = jnp.where(lane < 64, turned[tile], turned[tile + 1])
            mixed = jnp.where(lane < off - 80, left[tile + 1], mixed)
            mixed = jnp.where(lane >= off, left[tile], mixed)
        rows.append(roll_lanes(mixed, -off))
    return rows


def to_tiles(rows):
    lane = lane_index()
    turned_lane = jnp.where(lane < 64, lane + 64, lane - 64)
    placed = [roll_lanes(rows[y], 48 * y % 128) for y in range(8)]
    left, right = [], []
    for tile in range(3):
        a = c = None
        for y in range(8):
            lo, hi = max(48 * y, tile * 128), min(48 * y + 48, tile * 128 + 128)
            if lo >= hi:
                continue
            if a is None:
                a = c = placed[y]
            else:
                a = jnp.where(lane < lo - tile * 128, a, placed[y])
                c = jnp.where(turned_lane < lo - tile * 128, c, placed[y])
        left.append(a)
        right.append(roll_lanes(c, 64))
    return left, right


def three_terms(v):
    parts = []
    for _ in range(3):
        part = v.astype(BF16).astype(F32)
        parts.append(part)
        v = v - part
    return parts


def invert_factor(r, out):
    lane = lax.broadcasted_iota(jnp.int32, (8, 128), 1)
    sub = lax.broadcasted_iota(jnp.int32, (8, 128), 0)
    splat = lambda v, i, j: jnp.broadcast_to(v[i:i + 1, j:j + 1], (8, 128))
    spread = lambda v, i: jnp.broadcast_to(v[i:i + 1], (8, 128))

    def body(first_row, k):
        rows = pl.ds(pl.multiple_of(8 * k, 8), 8)
        top = [r[rows, 0:128], r[rows, 128:256]]
        off = 8 * lax.rem(k, 16)
        block = pltpu.roll(jnp.where(k >= 16, top[1], top[0]), lax.rem(128 - off, 128), 1)
        s = {(i, j): splat(block, j, i) for i in range(8) for j in range(i + 1)}
        recip, low = [], {}
        for col in range(8):
            recip.append(1.0 / s[col, col])
            for i in range(col + 1, 8):
                low[i, col] = s[i, col] * recip[col]
            for i in range(col + 1, 8):
                for j in range(col + 1, i + 1):
                    s[i, j] = s[i, j] - low[i, col] * s[j, col]
        inv = {}
        for j in range(8):
            for i in range(j + 1, 8):
                t = low[i, j]
                for p in range(j + 1, i):
                    t = t + low[i, p] * inv[p, j]
                inv[i, j] = -t
        cols, cols_t = [], []
        for j in range(8):
            v = jnp.where(sub == j, 1.0, 0.0)
            for i in range(j + 1, 8):
                v = jnp.where(sub == i, inv[i, j], v)
            cols.append(v)
            w = jnp.where(sub == j, 1.0, 0.0)
            for i in range(j):
                w = jnp.where(sub == i, inv[j, i], w)
            cols_t.append(w)
        pivot = recip[0]
        for i in range(1, 8):
            pivot = jnp.where(sub == i, recip[i], pivot)
        zs, ss = [], []
        for t in range(2):
            local = lane + 128 * t - 8 * k
            inside = jnp.logical_and(local >= 0, local < 8)
            v = jnp.where(inside, jnp.where(local == sub, 1.0, 0.0), top[t])
            y = cols[0] * spread(v, 0)
            for j in range(1, 8):
                y = y + cols[j] * spread(v, j)
            out[rows, 128 * t:128 * t + 128] = jnp.where(local < 8, y * jnp.sqrt(pivot), 0.0)
            y = y * pivot
            z = cols_t[0] * spread(y, 0)
            for j in range(1, 8):
                z = z + cols_t[j] * spread(y, j)
            zs.append(z)
            ss.append(jnp.where(local < 8, 0.0, top[t]))
        z, w = three_terms(jnp.concatenate(zs, 1)), three_terms(jnp.concatenate(ss, 1))
        left = jnp.concatenate([w[0], w[0], w[1], w[0], w[1], w[2]], 0).astype(BF16)
        right = jnp.concatenate([z[0], z[1], z[0], z[2], z[1], z[0]], 0).astype(BF16)
        live = slice(8 * first_row, M)
        update = lax.dot_general(left[:, live], right, (((0,), (0,)), ((), ())),
                                 preferred_element_type=F32)
        local = lax.broadcasted_iota(jnp.int32, (M - 8 * first_row, 256), 1) - 8 * k
        inside = jnp.logical_and(local >= 0, local < 8)
        r[live, :] = jnp.where(inside, 0.0, r[live, :]) - update

    for part in range(3):
        def segment(k, c):
            body(8 * part, k)
            return c
        lax.fori_loop(8 * part, 8 * part + 8, segment, 0)


def kernel(x_ref, p_ref, w_hbm, c_hbm, out_ref, recv, pot_in, w_ref, c_ref, field_a, field_b, pot, pack,
           own, part, rs_buf, xy_buf, sums, gsum, packed, work, inv_ref, rot, send_sems, recv_sems):
    b = lax.axis_index("band")
    d = lax.axis_index("dom")
    core = lax.rem(b, 2)
    y_pos, zh, x_pos = d // 8, lax.rem(d // 4, 2), lax.rem(d, 4)
    two = lax.rem(core + d, 2) == 0
    first = 3 * (d // 2) + lax.rem(d, 2) * (2 - core)
    me = d * 4 + b
    partner = b + 1 - 2 * core

    def remote(src, dst, send, receive, to_b, to_d):
        pltpu.make_async_remote_copy(
            src_ref=src, dst_ref=dst, send_sem=send_sems.at[send], recv_sem=recv_sems.at[receive],
            device_id=(to_b, to_d), device_id_type=MESH).start()

    def local(src, dst, receive):
        pltpu.make_async_copy(src, dst, recv_sems.at[receive]).start()

    def arrived(ref, receive):
        pltpu.make_async_copy(ref, ref, recv_sems.at[receive]).wait()

    def drain(ref, sem, times):
        def body(i, c):
            pltpu.make_async_copy(ref, ref, sem).wait()
            return c
        lax.fori_loop(0, times, body, 0)

    barrier = pltpu.get_barrier_semaphore()

    def greet(i, c):
        to = lax.rem(me + i, 128)
        pl.semaphore_signal(barrier, inc=1, device_id=(lax.rem(to, 4), to // 4), device_id_type=MESH)
        return c

    lax.fori_loop(1, 128, greet, 0)
    pl.semaphore_wait(barrier, 127)

    half = p_ref.at[:, pl.ds(pl.multiple_of(1152 * core, 128), 1152)]
    half_dst = pot_in.at[core, lax.rem(d, 4), :, d // 4, :]

    def send_potential(i, c):
        remote(half, half_dst, 1, 2, b, lax.rem(d + i, 32))
        return c

    local(half, half_dst, 2)
    lax.fori_loop(1, 32, send_potential, 0)

    def send_orbital(slot):
        def send(i, c):
            to = lax.rem(d + i, 32)
            to_two = lax.rem(core + to, 2) == 0
            o = 3 * (to // 2) + lax.rem(to, 2) * (2 - core) + slot
            src = x_ref.at[:, o, :]
            dst = recv.at[slot, lax.rem(d, 4), :, d // 4, :]

            def start():
                remote(src, dst, 0, slot, b, to)

            if slot == 0:
                start()
            else:
                pl.when(to_two)(start)
            return c

        def keep():
            local(x_ref.at[:, first + slot, :], recv.at[slot, lax.rem(d, 4), :, d // 4, :], slot)

        if slot == 0:
            keep()
        else:
            pl.when(two)(keep)
        lax.fori_loop(1, 32, send, 0)

    send_orbital(0)
    send_orbital(1)
    local(w_hbm, w_ref, 12)
    local(c_hbm, c_ref, 13)

    def unpack(load, store):
        def body(n, c):
            yb, q = n // 4, lax.rem(n, 4)
            for j in range(3):
                rows = to_rows(load(0, yb, q, j), load(1, yb, q, j))
                for y in range(8):
                    store(yb * 8 + y, pl.ds(pl.multiple_of(q * 24 + 8 * j, 8), 8), rows[y])
            return c

        lax.fori_loop(0, 12, body, 0)

    def chunk(start, t):
        return pl.ds(pl.multiple_of(start + 128 * t, 128), 128)

    def load_potential(side, yb, q, j):
        return [pot_in[side, q, j, :, chunk(yb * 384, t)] for t in range(3)]

    def store_potential(y, rows, v):
        pot[y, rows, :] = SCALE * v + DIAGONAL

    arrived(pot_in.at[core], 2)
    remote(pot_in.at[core], pot_in.at[core], 7, 11, partner, d)
    arrived(pot_in.at[core], 11)
    unpack(load_potential, store_potential)

    def halo(field):
        def body(i, c):
            for r in range(12):
                rows = pl.ds(8 * r, 8)
                field[30 + i, rows, :] = pltpu.roll(field[6 + i, rows, :], 64, 1)
                field[i, rows, :] = pltpu.roll(field[24 + i, rows, :], 64, 1)
            return c

        lax.fori_loop(0, 6, body, 0)

    def step(src, dst, is_first):
        def block(n, c):
            y0 = n * ROWS + 6
            values = src[pl.ds(y0, ROWS)].reshape(ROWS * 96, 128)
            high = values.astype(BF16)
            low = (values - high.astype(F32)).astype(BF16)
            along_z = jnp.dot(jnp.concatenate([high, low], 1), w_ref[...], preferred_element_type=F32)
            along_x = []
            for r in range(0, ROWS, 2):
                one, other = slice(96 * r, 96 * r + 96), slice(96 * r + 96, 96 * r + 192)
                columns = jnp.concatenate([jnp.concatenate([high[one], high[other]], 1),
                                           jnp.concatenate([low[one], low[other]], 1)], 0)
                along_x.append(jnp.dot(c_ref[...], columns, preferred_element_type=F32))
            for r in range(ROWS):
                for i in range(12):
                    rows = pl.ds(8 * i, 8)
                    acc = src[y0 + r, rows, :] * pot[y0 + r - 6, rows, :]
                    for k in range(1, 7):
                        acc = acc + COEFS[k] * (src[y0 + r + k, rows, :] + src[y0 + r - k, rows, :])
                    z = along_z[96 * r + 8 * i:96 * r + 8 * i + 8]
                    half_lanes = slice(128 * (r % 2), 128 * (r % 2) + 128)
                    x = (along_x[r // 2][8 * i:8 * i + 8, half_lanes]
                         + along_x[r // 2][96 + 8 * i:96 + 8 * i + 8, half_lanes])
                    acc = acc + ((z[:, :128] + z[:, 128:]) + x)
                    dst[y0 + r, rows, :] = 0.5 * acc if is_first else acc - dst[y0 + r, rows, :]
            return c

        lax.fori_loop(0, 24 // ROWS, block, 0)

    def quarter(band):
        return 14 * band - jnp.maximum(band - 1, 0)

    def spread(slot):
        def send(i, c):
            to = lax.rem(me + i, 128)
            to_b, to_d = lax.rem(to, 4), to // 4
            src = pack.at[slot, lax.rem(to_d, 4), pl.ds(quarter(to_b), TILES), to_d // 4, :]
            remote(src, own.at[:, 48 * b + first + slot, :], 2, 3, to_b, to_d)
            return c

        lax.fori_loop(1, 128, send, 0)
        local(pack.at[slot, lax.rem(d, 4), pl.ds(quarter(b), TILES), d // 4, :],
              own.at[:, 48 * b + first + slot, :], 3)

    def filter_orbital(slot):
        def load(side, yb, q, j):
            return [recv[slot, q, j, :, chunk(yb * 384 + 1152 * side, t)] for t in range(3)]

        def store(y, rows, v):
            field_a[y + 6, rows, :] = v

        def repack(n, c):
            yb, q = n // 4, lax.rem(n, 4)
            for j in range(3):
                rows = [field_a[6 + yb * 8 + y, pl.ds(pl.multiple_of(q * 24 + 8 * j, 8), 8), :] for y in range(8)]
                left, right = to_tiles(rows)
                for t in range(3):
                    pack[slot, q, j * 18 + yb * 3 + t] = left[t]
                    pack[slot, q, j * 18 + 9 + yb * 3 + t] = right[t]
            return c

        arrived(recv.at[slot], slot)
        unpack(load, store)
        halo(field_a)
        step(field_a, field_b, True)
        halo(field_b)
        step(field_b, field_a, False)
        halo(field_a)
        step(field_a, field_b, False)
        halo(field_b)
        step(field_b, field_a, False)
        lax.fori_loop(0, 12, repack, 0)
        spread(slot)

    arrived(w_ref, 12)
    arrived(c_ref, 13)
    filter_orbital(0)
    pl.when(two)(lambda: filter_orbital(1))
    arrived(own, 3)

    total = jnp.zeros((M, M), F32)
    for i in range(0, TILES, 2):
        one = own[i]
        if i == 0:
            one = jnp.where(b >= 2, 0.0, one)
        both = jnp.concatenate([one, own[i + 1]], 1)
        total = total + lax.dot_general(both, both, (((1,), (1,)), ((), ())), precision=lax.Precision.HIGHEST,
                                        preferred_element_type=F32)
    near = total[:, :128]
    far = jnp.concatenate([total[:, 128:], jnp.zeros((M, 64), F32)], 1)
    left_half = lax.broadcasted_iota(jnp.int32, (64, 128), 1) < 64
    packed[0:64] = near[0:64]
    packed[64:128] = jnp.where(left_half, far[0:64], near[64:128])
    packed[128:192] = jnp.where(left_half, far[64:128], pltpu.roll(far[128:192], 64, 1))
    for i in range(8):
        part[i] = packed[24 * i:24 * i + 24]

    mine = zh * 4 + b
    for i in range(1, 8):
        to = lax.rem(mine + i, 8)
        remote(part.at[to], rs_buf.at[mine], 4, 4, lax.rem(to, 4), y_pos * 8 + (to // 4) * 4 + x_pos)
    rs_buf[mine] = part[mine]
    arrived(rs_buf.at[pl.ds(0, 7)], 4)
    acc = rs_buf[0]
    for i in range(1, 8):
        acc = acc + rs_buf[i]
    sums[...] = acc
    spot = y_pos * 4 + x_pos
    for i in range(1, 16):
        to = lax.rem(spot + i, 16)
        remote(sums, xy_buf.at[spot], 5, 5, b, (to // 4) * 8 + zh * 4 + lax.rem(to, 4))
    xy_buf[spot] = acc
    arrived(xy_buf.at[pl.ds(0, 15)], 5)
    acc = xy_buf[0]
    for i in range(1, 16):
        acc = acc + xy_buf[i]
    acc = acc / CELLS
    gsum[mine] = acc
    for i in range(1, 8):
        to = lax.rem(mine + i, 8)
        remote(gsum.at[mine], gsum.at[mine], 6, 6, lax.rem(to, 4), y_pos * 8 + (to // 4) * 4 + x_pos)
    arrived(gsum.at[pl.ds(0, 7)], 6)

    for i in range(8):
        packed[24 * i:24 * i + 24] = gsum[i]
    work[0:64, 0:128] = packed[0:64]
    work[0:64, 128:256] = packed[64:128]
    work[64:128, 0:128] = packed[64:128]
    work[64:128, 128:256] = packed[128:192]
    work[128:192, 0:128] = packed[128:192]
    work[128:192, 128:256] = pltpu.roll(packed[128:192], 64, 1)
    invert_factor(work, inv_ref)

    def rotate(n, c):
        columns = jnp.concatenate([own[2 * n], own[2 * n + 1]], 1)
        product = jnp.dot(inv_ref[:, 0:M], columns, precision=lax.Precision.HIGHEST, preferred_element_type=F32)
        for i in range(2):
            tile = quarter(b) + 2 * n + i
            place = out_ref.at[tile // 18, :, pl.ds(pl.multiple_of(128 * lax.rem(tile, 18), 128), 128)]
            for band in range(4):
                rot[2 * n + i, band] = product[48 * band:48 * band + 48, 128 * i:128 * i + 128]

            @pl.when(jnp.logical_or(b < 2, 2 * n + i > 0))
            def _():
                for away in (2, 3, 1):
                    to = lax.rem(b + away, 4)
                    remote(rot.at[2 * n + i, to], place, 8, 7 + b, to, d)
                local(rot.at[2 * n + i, b], place, 7 + b)
        return c

    lax.fori_loop(0, TILES // 2, rotate, 0)

    tile = rot.at[0, 0]
    mine_tiles = jnp.where(b < 2, 14, 13)
    for band in range(4):
        arrived(rot.at[pl.ds(0, 14 if band < 2 else 13), 0], 7 + band)
    drain(tile, send_sems.at[8], 3 * mine_tiles)
    orbital = recv.at[0, 0, :, 0, :]
    drain(orbital, send_sems.at[0], jnp.where(two, 46, 47))
    drain(half_dst, send_sems.at[1], 31)
    drain(pot_in.at[0], send_sems.at[7], 1)
    share = pack.at[0, 0, pl.ds(0, TILES), 0, :]
    drain(share, send_sems.at[2], jnp.where(two, 254, 127))
    drain(sums, send_sems.at[4], 7)
    drain(sums, send_sems.at[5], 15)
    drain(sums, send_sems.at[6], 7)


def per_device(orbitals, potential):
    anywhere = pl.BlockSpec(memory_space=pl.ANY)
    out = pl.pallas_call(
        kernel,
        out_shape=jax.ShapeDtypeStruct((3, 48, 2304), F32),
        in_specs=[anywhere] * 4,
        out_specs=pl.BlockSpec(memory_space=pltpu.VMEM),
        scratch_shapes=[
            pltpu.VMEM((2, 4, 3, 8, 2304), F32),
            pltpu.VMEM((2, 4, 3, 8, 1152), F32),
            pltpu.VMEM((256, 256), BF16),
            pltpu.VMEM((192, 192), BF16),
            pltpu.VMEM((36, 96, 128), F32),
            pltpu.VMEM((36, 96, 128), F32),
            pltpu.VMEM((24, 96, 128), F32),
            pltpu.VMEM((2, 4, 54, 8, 128), F32),
            pltpu.VMEM((TILES, M, 128), F32),
            pltpu.VMEM((8, 24, 128), F32),
            pltpu.VMEM((8, 24, 128), F32),
            pltpu.VMEM((16, 24, 128), F32),
            pltpu.VMEM((24, 128), F32),
            pltpu.VMEM((8, 24, 128), F32),
            pltpu.VMEM((M, 128), F32),
            pltpu.VMEM((M, 256), F32),
            pltpu.VMEM((M, 256), F32),
            pltpu.VMEM((TILES, 4, 48, 128), F32),
            pltpu.SemaphoreType.DMA((9,)),
            pltpu.SemaphoreType.DMA((14,)),
        ],
        compiler_params=pltpu.CompilerParams(
            collective_id=0, has_side_effects=True, vmem_limit_bytes=56 * 2**20),
    )(jnp.transpose(orbitals, (1, 0, 2)), potential, jnp.asarray(z_matrix()), jnp.asarray(x_matrix()))
    return jnp.transpose(out, (1, 0, 2))


def solution(mesh):
    placed = (P("band", "dom", None), P("dom", None))
    return jax.shard_map(
        per_device, mesh=mesh, in_specs=placed, out_specs=P("band", "dom", None), check_vma=False
    )
```

```python
import jax
import jax.numpy as jnp
import numpy as np
from jax import lax
from jax.experimental import pallas as pl
from jax.experimental.pallas import tpu as pltpu
from jax.sharding import PartitionSpec as P

M = 192
CELLS = 221184
MESH = pl.DeviceIdType.MESH
F32, BF16 = jnp.float32, jnp.bfloat16

stencil_weights = (
    -5369.0 / 1800.0,
    12.0 / 7.0,
    -15.0 / 56.0,
    10.0 / 189.0,
    -1.0 / 112.0,
    2.0 / 1925.0,
    -1.0 / 16632.0,
)
SCALE = 0.4
COEFS = [-0.5 * SCALE * w for w in stencil_weights]
DIAGONAL = 3.0 * COEFS[0] - 7.0 * SCALE
TILES = 14
EARLY = 8
ROWS = 8


def two_terms(full):
    high = full.astype(BF16)
    return high, (full - high.astype(np.float32)).astype(BF16)


def z_matrix():
    full = np.zeros((128, 128), np.float32)
    for half in range(2):
        for z in range(48):
            for k in range(1, 7):
                full[half * 64 + z, half * 64 + (z + k) % 48] += COEFS[k]
                full[half * 64 + z, half * 64 + (z - k) % 48] += COEFS[k]
    row = np.concatenate(two_terms(full), 1)
    return np.concatenate([row, row], 0)


def x_matrix():
    full = np.zeros((96, 96), np.float32)
    place = [(r % 8) * 12 + r // 8 for r in range(96)]
    for a in range(96):
        for c in range(96):
            away = (place[a] - place[c]) % 96
            away = min(away, 96 - away)
            if 1 <= away <= 6:
                full[a, c] = COEFS[away]
    high, low = two_terms(full)
    return np.concatenate([np.concatenate([high, high], 1), np.concatenate([low, low], 1)], 0)


def roll_lanes(v, by):
    by = by % 128
    return v if by == 0 else pltpu.roll(v, by, 1)


def lane_index():
    return lax.broadcasted_iota(jnp.int32, (8, 128), 1)


def to_rows(left, right):
    lane = lane_index()
    turned = [roll_lanes(v, 64) for v in right]
    rows = []
    for y in range(8):
        tile, off = 48 * y // 128, 48 * y % 128
        if off + 48 <= 128:
            inside = jnp.logical_and(lane >= off, lane < off + 48)
            mixed = jnp.where(inside, left[tile], turned[tile])
        else:
            mixed = jnp.where(lane < 64, turned[tile], turned[tile + 1])
            mixed = jnp.where(lane < off - 80, left[tile + 1], mixed)
            mixed = jnp.where(lane >= off, left[tile], mixed)
        rows.append(roll_lanes(mixed, -off))
    return rows


def to_tiles(rows):
    lane = lane_index()
    turned_lane = jnp.where(lane < 64, lane + 64, lane - 64)
    placed = [roll_lanes(rows[y], 48 * y % 128) for y in range(8)]
    left, right = [], []
    for tile in range(3):
        a = c = None
        for y in range(8):
            lo, hi = max(48 * y, tile * 128), min(48 * y + 48, tile * 128 + 128)
            if lo >= hi:
                continue
            if a is None:
                a = c = placed[y]
            else:
                a = jnp.where(lane < lo - tile * 128, a, placed[y])
                c = jnp.where(turned_lane < lo - tile * 128, c, placed[y])
        left.append(a)
        right.append(roll_lanes(c, 64))
    return left, right


def three_terms(v):
    parts = []
    for _ in range(3):
        part = v.astype(BF16).astype(F32)
        parts.append(part)
        v = v - part
    return parts


def invert_factor(r, out):
    lane = lax.broadcasted_iota(jnp.int32, (8, 128), 1)
    sub = lax.broadcasted_iota(jnp.int32, (8, 128), 0)
    splat = lambda v, i, j: jnp.broadcast_to(v[i:i + 1, j:j + 1], (8, 128))
    spread = lambda v, i: jnp.broadcast_to(v[i:i + 1], (8, 128))

    def body(first_row, k):
        rows = pl.ds(pl.multiple_of(8 * k, 8), 8)
        top = [r[rows, 0:128], r[rows, 128:256]]
        off = 8 * lax.rem(k, 16)
        block = pltpu.roll(jnp.where(k >= 16, top[1], top[0]), lax.rem(128 - off, 128), 1)
        s = {(i, j): splat(block, j, i) for i in range(8) for j in range(i + 1)}
        recip, low = [], {}
        for col in range(8):
            recip.append(1.0 / s[col, col])
            for i in range(col + 1, 8):
                low[i, col] = s[i, col] * recip[col]
            for i in range(col + 1, 8):
                for j in range(col + 1, i + 1):
                    s[i, j] = s[i, j] - low[i, col] * s[j, col]
        inv = {}
        for j in range(8):
            for i in range(j + 1, 8):
                t = low[i, j]
                for p in range(j + 1, i):
                    t = t + low[i, p] * inv[p, j]
                inv[i, j] = -t
        cols, cols_t = [], []
        for j in range(8):
            v = jnp.where(sub == j, 1.0, 0.0)
            for i in range(j + 1, 8):
                v = jnp.where(sub == i, inv[i, j], v)
            cols.append(v)
            w = jnp.where(sub == j, 1.0, 0.0)
            for i in range(j):
                w = jnp.where(sub == i, inv[j, i], w)
            cols_t.append(w)
        pivot = recip[0]
        for i in range(1, 8):
            pivot = jnp.where(sub == i, recip[i], pivot)
        zs, ss = [], []
        for t in range(2):
            local = lane + 128 * t - 8 * k
            inside = jnp.logical_and(local >= 0, local < 8)
            v = jnp.where(inside, jnp.where(local == sub, 1.0, 0.0), top[t])
            y = cols[0] * spread(v, 0)
            for j in range(1, 8):
                y = y + cols[j] * spread(v, j)
            out[rows, 128 * t:128 * t + 128] = jnp.where(local < 8, y * jnp.sqrt(pivot), 0.0)
            y = y * pivot
            z = cols_t[0] * spread(y, 0)
            for j in range(1, 8):
                z = z + cols_t[j] * spread(y, j)
            zs.append(z)
            ss.append(jnp.where(local < 8, 0.0, top[t]))
        z, w = three_terms(jnp.concatenate(zs, 1)), three_terms(jnp.concatenate(ss, 1))
        left = jnp.concatenate([w[0], w[0], w[1], w[0], w[1], w[2]], 0).astype(BF16)
        right = jnp.concatenate([z[0], z[1], z[0], z[2], z[1], z[0]], 0).astype(BF16)
        live = slice(8 * first_row, M)
        update = lax.dot_general(left[:, live], right, (((0,), (0,)), ((), ())),
                                 preferred_element_type=F32)
        local = lax.broadcasted_iota(jnp.int32, (M - 8 * first_row, 256), 1) - 8 * k
        inside = jnp.logical_and(local >= 0, local < 8)
        r[live, :] = jnp.where(inside, 0.0, r[live, :]) - update

    for part in range(3):
        def segment(k, c):
            body(8 * part, k)
            return c
        lax.fori_loop(8 * part, 8 * part + 8, segment, 0)


def kernel(x_ref, p_ref, w_hbm, c_hbm, out_ref, recv, pot_in, w_ref, c_ref, field_a, field_b, pot, pack,
           own, part, rs_buf, xy_buf, sums, gsum, packed, work, inv_ref, rot, gathered, send_sems, recv_sems, ready):
    b = lax.axis_index("band")
    d = lax.axis_index("dom")
    core = lax.rem(b, 2)
    y_pos, zh, x_pos = d // 8, lax.rem(d // 4, 2), lax.rem(d, 4)
    two = lax.rem(core + d, 2) == 0
    first = 3 * (d // 2) + lax.rem(d, 2) * (2 - core)
    me = d * 4 + b
    partner = b + 1 - 2 * core

    def remote(src, dst, send, receive, to_b, to_d):
        pltpu.make_async_remote_copy(
            src_ref=src, dst_ref=dst, send_sem=send_sems.at[send], recv_sem=recv_sems.at[receive],
            device_id=(to_b, to_d), device_id_type=MESH).start()

    def local(src, dst, receive):
        pltpu.make_async_copy(src, dst, recv_sems.at[receive]).start()

    def arrived(ref, receive):
        pltpu.make_async_copy(ref, ref, recv_sems.at[receive]).wait()

    def drain(ref, sem, times):
        def body(i, c):
            pltpu.make_async_copy(ref, ref, sem).wait()
            return c
        lax.fori_loop(0, times, body, 0)

    barrier = pltpu.get_barrier_semaphore()

    def greet(i, c):
        pl.semaphore_signal(barrier, inc=1, device_id=(b, lax.rem(d + i, 32)), device_id_type=MESH)
        return c

    def greet_again(i, c):
        pl.semaphore_signal(ready, inc=1, device_id=(b, lax.rem(d + i, 32)), device_id_type=MESH)
        return c

    lax.fori_loop(1, 32, greet, 0)
    for i in range(1, 4):
        pl.semaphore_signal(barrier, inc=1, device_id=(lax.rem(b + i, 4), d), device_id_type=MESH)
    pl.semaphore_wait(barrier, 34)

    half = p_ref.at[:, pl.ds(pl.multiple_of(1152 * core, 128), 1152)]
    half_dst = pot_in.at[core, lax.rem(d, 4), :, d // 4, :]

    def send_potential(i, c):
        remote(half, half_dst, 1, 2, b, lax.rem(d + i, 32))
        return c

    def send_orbital(slot):
        def send(i, c):
            to = lax.rem(d + i, 32)
            to_two = lax.rem(core + to, 2) == 0
            o = 3 * (to // 2) + lax.rem(to, 2) * (2 - core) + slot
            src = x_ref.at[:, o, :]
            dst = recv.at[slot, lax.rem(d, 4), :, d // 4, :]

            def start():
                remote(src, dst, 0, slot, b, to)

            if slot == 0:
                start()
            else:
                pl.when(to_two)(start)
            return c

        def keep():
            local(x_ref.at[:, first + slot, :], recv.at[slot, lax.rem(d, 4), :, d // 4, :], slot)

        if slot == 0:
            keep()
        else:
            pl.when(two)(keep)
        lax.fori_loop(1, 32, send, 0)

    send_orbital(0)
    local(half, half_dst, 2)
    lax.fori_loop(1, 32, send_potential, 0)
    lax.fori_loop(1, 32, greet_again, 0)
    local(w_hbm, w_ref, 12)
    local(c_hbm, c_ref, 13)
    pot[...] = jnp.full(pot.shape, DIAGONAL, F32)

    def unpack(load, store):
        def body(n, c):
            yb, q = n // 4, lax.rem(n, 4)
            for j in range(3):
                rows = to_rows(load(0, yb, q, j), load(1, yb, q, j))
                for y in range(8):
                    store(yb * 8 + y, pl.ds(pl.multiple_of(q * 24 + 8 * j, 8), 8), rows[y])
            return c

        lax.fori_loop(0, 12, body, 0)

    def chunk(start, t):
        return pl.ds(pl.multiple_of(start + 128 * t, 128), 128)

    def load_potential(side, yb, q, j):
        return [pot_in[side, q, j, :, chunk(yb * 384, t)] for t in range(3)]

    def put(field, y, rows, v):
        field[y, rows, :] = v
        field[24 + y, rows, :] = pltpu.roll(v, 64, 1)

    def store_potential(y, rows, v):
        v = SCALE * v
        pot[y, rows, :] = v + DIAGONAL
        put(field_b, y, rows, field_b[y, rows, :] + (0.5 * v) * field_a[y, rows, :])

    def step(src, dst, weight):
        def block(n, c):
            y0 = n * ROWS
            values = src[pl.ds(y0, ROWS)].reshape(ROWS * 96, 128)
            high = values.astype(BF16)
            low = (values - high.astype(F32)).astype(BF16)
            along_z = jnp.dot(jnp.concatenate([high, low], 1), w_ref[...], preferred_element_type=F32)
            along_x = []
            for r in range(0, ROWS, 2):
                one, other = slice(96 * r, 96 * r + 96), slice(96 * r + 96, 96 * r + 192)
                columns = jnp.concatenate([jnp.concatenate([high[one], high[other]], 1),
                                           jnp.concatenate([low[one], low[other]], 1)], 0)
                along_x.append(jnp.dot(c_ref[...], columns, preferred_element_type=F32))
            at = [lax.rem(y0 + 48 + s, 48) for s in range(-6, ROWS + 6)]
            for i in range(12):
                rows = pl.ds(8 * i, 8)
                near = [src[y, rows, :] for y in at]
                for r in range(ROWS):
                    acc = near[6 + r] * pot[y0 + r, rows, :]
                    for k in range(1, 7):
                        acc = acc + COEFS[k] * (near[6 + r + k] + near[6 + r - k])
                    z = along_z[96 * r + 8 * i:96 * r + 8 * i + 8]
                    half_lanes = slice(128 * (r % 2), 128 * (r % 2) + 128)
                    x = (along_x[r // 2][8 * i:8 * i + 8, half_lanes]
                         + along_x[r // 2][96 + 8 * i:96 + 8 * i + 8, half_lanes])
                    acc = acc + ((z[:, :128] + z[:, 128:]) + x)
                    put(dst, y0 + r, rows, weight * acc - dst[y0 + r, rows, :])
            return c

        lax.fori_loop(0, 24 // ROWS, block, 0)

    def quarter(band):
        return 14 * band - jnp.maximum(band - 1, 0)

    def spread(slot):
        def send(i, c):
            to = lax.rem(me + i, 128)
            to_b, to_d = lax.rem(to, 4), to // 4
            src = pack.at[slot, lax.rem(to_d, 4), pl.ds(quarter(to_b), TILES), to_d // 4, :]
            remote(src, own.at[:, 48 * b + first + slot, :], 2, 3, to_b, to_d)
            return c

        lax.fori_loop(1, 128, send, 0)
        local(pack.at[slot, lax.rem(d, 4), pl.ds(quarter(b), TILES), d // 4, :],
              own.at[:, 48 * b + first + slot, :], 3)

    def add_potential():
        arrived(pot_in.at[core], 2)
        remote(pot_in.at[core], pot_in.at[core], 7, 11, partner, d)
        arrived(pot_in.at[core], 11)
        unpack(load_potential, store_potential)

    def send_second():
        send_orbital(1)

    def filter_orbital(slot, c):
        def load(side, yb, q, j):
            return [recv[slot, q, j, :, chunk(yb * 384 + 1152 * side, t)] for t in range(3)]

        def store(y, rows, v):
            put(field_a, y, rows, v)
            field_b[y, rows, :] = jnp.zeros_like(v)

        def repack(n, c):
            yb, q = n // 4, lax.rem(n, 4)
            for j in range(3):
                rows = [field_a[yb * 8 + y, pl.ds(pl.multiple_of(q * 24 + 8 * j, 8), 8), :] for y in range(8)]
                left, right = to_tiles(rows)
                for t in range(3):
                    pack[slot, q, j * 18 + yb * 3 + t] = left[t]
                    pack[slot, q, j * 18 + 9 + yb * 3 + t] = right[t]
            return c

        arrived(recv.at[slot], slot)
        pl.when(slot == 0)(send_second)
        unpack(load, store)

        def steps(t, c):
            step(field_a, field_b, jnp.where(t == 0, 0.5, 1.0))
            pl.when(jnp.logical_and(slot == 0, t == 0))(add_potential)
            step(field_b, field_a, 1.0)
            return c

        lax.fori_loop(0, 2, steps, 0)

        @pl.when(slot == 0)
        def _():
            pl.semaphore_wait(ready, 31)

        lax.fori_loop(0, 12, repack, 0)
        spread(slot)
        return c

    arrived(w_ref, 12)
    arrived(c_ref, 13)
    lax.fori_loop(0, jnp.where(two, 2, 1), filter_orbital, 0)
    arrived(own, 3)

    z_peer = lax.rem(b + 2, 4)
    other = lax.rem(partner + 2, 4)
    PART = EARLY // 2

    def exchange(i):
        tiles = pl.ds(PART * i, PART)
        remote(own.at[tiles], gathered.at[1, tiles], 9, 14 + i, z_peer, d)

    def forward(i):
        tiles = pl.ds(PART * i, PART)
        arrived(gathered.at[1, tiles], 14 + i)
        remote(gathered.at[1, tiles], gathered.at[2, tiles], 11, 17 + i, partner, d)

    total = jnp.zeros((M, M), F32)
    for i in range(0, TILES, 2):
        one = own[i]
        if i == 0:
            one = jnp.where(b >= 2, 0.0, one)
        both = jnp.concatenate([one, own[i + 1]], 1)
        total = total + lax.dot_general(both, both, (((1,), (1,)), ((), ())), precision=lax.Precision.HIGHEST,
                                        preferred_element_type=F32)
    near = total[:, :128]
    far = jnp.concatenate([total[:, 128:], jnp.zeros((M, 64), F32)], 1)
    left_half = lax.broadcasted_iota(jnp.int32, (64, 128), 1) < 64
    packed[0:64] = near[0:64]
    packed[64:128] = jnp.where(left_half, far[0:64], near[64:128])
    packed[128:192] = jnp.where(left_half, far[64:128], pltpu.roll(far[128:192], 64, 1))
    for i in range(8):
        part[i] = packed[24 * i:24 * i + 24]

    mine = zh * 4 + b
    for i in range(1, 8):
        to = lax.rem(mine + i, 8)
        remote(part.at[to], rs_buf.at[mine], 4, 4, lax.rem(to, 4), y_pos * 8 + (to // 4) * 4 + x_pos)
    rs_buf[mine] = part[mine]
    arrived(rs_buf.at[pl.ds(0, 7)], 4)
    exchange(0)
    acc = rs_buf[0]
    for i in range(1, 8):
        acc = acc + rs_buf[i]
    sums[...] = acc
    spot = y_pos * 4 + x_pos
    for i in range(1, 16):
        to = lax.rem(spot + i, 16)
        remote(sums, xy_buf.at[spot], 5, 5, b, (to // 4) * 8 + zh * 4 + lax.rem(to, 4))
    xy_buf[spot] = acc
    arrived(xy_buf.at[pl.ds(0, 15)], 5)
    acc = xy_buf[0]
    for i in range(1, 16):
        acc = acc + xy_buf[i]
    acc = acc / CELLS
    gsum[mine] = acc
    for i in range(1, 8):
        to = lax.rem(mine + i, 8)
        remote(gsum.at[mine], gsum.at[mine], 6, 6, lax.rem(to, 4), y_pos * 8 + (to // 4) * 4 + x_pos)
    arrived(gsum.at[pl.ds(0, 7)], 6)

    exchange(1)
    remote(own.at[pl.ds(0, EARLY)], gathered.at[0, pl.ds(0, EARLY)], 10, 16, partner, d)
    for i in range(8):
        packed[24 * i:24 * i + 24] = gsum[i]
    work[0:64, 0:128] = packed[0:64]
    work[0:64, 128:256] = packed[64:128]
    work[64:128, 0:128] = packed[64:128]
    work[64:128, 128:256] = packed[128:192]
    work[128:192, 0:128] = packed[128:192]
    work[128:192, 128:256] = pltpu.roll(packed[128:192], 64, 1)
    invert_factor(work, inv_ref)

    def place(tile):
        return tile // 18, pl.ds(pl.multiple_of(128 * lax.rem(tile, 18), 128), 128)

    def product(rows, block, n):
        columns = jnp.concatenate([block[2 * n], block[2 * n + 1]], 1)
        return jnp.dot(rows, columns, precision=lax.Precision.HIGHEST, preferred_element_type=F32)

    def rotate(n, c):
        result = product(inv_ref[:, 0:M], own, EARLY // 2 + n)
        for i in range(2):
            plane, lanes = place(quarter(b) + EARLY + 2 * n + i)
            for band in range(4):
                rot[2 * n + i, band] = result[48 * band:48 * band + 48, 128 * i:128 * i + 128]
            for away in (2, 3, 1):
                to = lax.rem(b + away, 4)
                remote(rot.at[2 * n + i, to], out_ref.at[plane, :, lanes], 8, 7 + b, to, d)
            local(rot.at[2 * n + i, b], out_ref.at[plane, :, lanes], 7 + b)
        return c

    def rotate_early(block, band):
        def body(n, c):
            result = product(inv_ref[pl.ds(pl.multiple_of(48 * b, 8), 48), 0:M], block, n)
            for i in range(2):
                plane, lanes = place(quarter(band) + 2 * n + i)

                def keep():
                    out_ref[plane, :, lanes] = result[:, 128 * i:128 * i + 128]

                if i == 0:
                    pl.when(jnp.logical_or(band < 2, n > 0))(keep)
                else:
                    keep()
            return c

        lax.fori_loop(0, EARLY // 2, body, 0)

    lax.fori_loop(0, (TILES - EARLY) // 2, rotate, 0)
    forward(0)
    forward(1)
    rotate_early(own, b)
    arrived(gathered.at[0, pl.ds(0, EARLY)], 16)
    rotate_early(gathered.at[0], partner)
    rotate_early(gathered.at[1], z_peer)
    for i in range(2):
        arrived(gathered.at[2, pl.ds(PART * i, PART)], 17 + i)
    rotate_early(gathered.at[2], other)

    late = TILES - EARLY
    for band in range(4):
        arrived(rot.at[pl.ds(0, late), 0], 7 + band)
    drain(rot.at[0, 0], send_sems.at[8], 3 * late)
    drain(gathered.at[0, pl.ds(0, PART)], send_sems.at[9], 2)
    drain(gathered.at[0, pl.ds(0, EARLY)], send_sems.at[10], 1)
    drain(gathered.at[0, pl.ds(0, PART)], send_sems.at[11], 2)
    orbital = recv.at[0, 0, :, 0, :]
    drain(orbital, send_sems.at[0], jnp.where(two, 46, 47))
    drain(half_dst, send_sems.at[1], 31)
    drain(pot_in.at[0], send_sems.at[7], 1)
    share = pack.at[0, 0, pl.ds(0, TILES), 0, :]
    drain(share, send_sems.at[2], jnp.where(two, 254, 127))
    drain(sums, send_sems.at[4], 7)
    drain(sums, send_sems.at[5], 15)
    drain(sums, send_sems.at[6], 7)


def per_device(orbitals, potential):
    anywhere = pl.BlockSpec(memory_space=pl.ANY)
    out = pl.pallas_call(
        kernel,
        out_shape=jax.ShapeDtypeStruct((3, 48, 2304), F32),
        in_specs=[anywhere] * 4,
        out_specs=pl.BlockSpec(memory_space=pltpu.VMEM),
        scratch_shapes=[
            pltpu.VMEM((2, 4, 3, 8, 2304), F32),
            pltpu.VMEM((2, 4, 3, 8, 1152), F32),
            pltpu.VMEM((256, 256), BF16),
            pltpu.VMEM((192, 192), BF16),
            pltpu.VMEM((48, 96, 128), F32),
            pltpu.VMEM((48, 96, 128), F32),
            pltpu.VMEM((24, 96, 128), F32),
            pltpu.VMEM((2, 4, 54, 8, 128), F32),
            pltpu.VMEM((TILES, M, 128), F32),
            pltpu.VMEM((8, 24, 128), F32),
            pltpu.VMEM((8, 24, 128), F32),
            pltpu.VMEM((16, 24, 128), F32),
            pltpu.VMEM((24, 128), F32),
            pltpu.VMEM((8, 24, 128), F32),
            pltpu.VMEM((M, 128), F32),
            pltpu.VMEM((M, 256), F32),
            pltpu.VMEM((M, 256), F32),
            pltpu.VMEM((TILES - EARLY, 4, 48, 128), F32),
            pltpu.VMEM((3, EARLY, M, 128), F32),
            pltpu.SemaphoreType.DMA((12,)),
            pltpu.SemaphoreType.DMA((20,)),
            pltpu.SemaphoreType.REGULAR,
        ],
        compiler_params=pltpu.CompilerParams(
            collective_id=0, has_side_effects=True, vmem_limit_bytes=56 * 2**20),
    )(jnp.transpose(orbitals, (1, 0, 2)), potential, jnp.asarray(z_matrix()), jnp.asarray(x_matrix()))
    return jnp.transpose(out, (1, 0, 2))


def solution(mesh):
    placed = (P("band", "dom", None), P("dom", None))
    return jax.shard_map(
        per_device, mesh=mesh, in_specs=placed, out_specs=P("band", "dom", None), check_vma=False
    )
```

```python
import jax
import jax.numpy as jnp
import numpy as np
from jax import lax
from jax.experimental import pallas as pl
from jax.experimental.pallas import tpu as pltpu
from jax.sharding import PartitionSpec as P

M = 192
CELLS = 221184
MESH = pl.DeviceIdType.MESH
F32, BF16 = jnp.float32, jnp.bfloat16

stencil_weights = (
    -5369.0 / 1800.0,
    12.0 / 7.0,
    -15.0 / 56.0,
    10.0 / 189.0,
    -1.0 / 112.0,
    2.0 / 1925.0,
    -1.0 / 16632.0,
)
SCALE = 0.4
COEFS = [-0.5 * SCALE * w for w in stencil_weights]
DIAGONAL = 3.0 * COEFS[0] - 7.0 * SCALE
TILES = 14
EARLY = 8
ROWS = 8


def two_terms(full):
    high = full.astype(BF16)
    return high, (full - high.astype(np.float32)).astype(BF16)


def z_matrix():
    full = np.zeros((128, 128), np.float32)
    for half in range(2):
        for z in range(48):
            for k in range(1, 7):
                full[half * 64 + z, half * 64 + (z + k) % 48] += COEFS[k]
                full[half * 64 + z, half * 64 + (z - k) % 48] += COEFS[k]
    row = np.concatenate(two_terms(full), 1)
    return np.concatenate([row, row], 0)


def x_matrix():
    full = np.zeros((96, 96), np.float32)
    place = [(r % 8) * 12 + r // 8 for r in range(96)]
    for a in range(96):
        for c in range(96):
            away = (place[a] - place[c]) % 96
            away = min(away, 96 - away)
            if 1 <= away <= 6:
                full[a, c] = COEFS[away]
    high, low = two_terms(full)
    return np.concatenate([np.concatenate([high, high], 1), np.concatenate([low, low], 1)], 0)


def roll_lanes(v, by):
    by = by % 128
    return v if by == 0 else pltpu.roll(v, by, 1)


def lane_index():
    return lax.broadcasted_iota(jnp.int32, (8, 128), 1)


def to_rows(left, right):
    lane = lane_index()
    turned = [roll_lanes(v, 64) for v in right]
    rows = []
    for y in range(8):
        tile, off = 48 * y // 128, 48 * y % 128
        if off + 48 <= 128:
            inside = jnp.logical_and(lane >= off, lane < off + 48)
            mixed = jnp.where(inside, left[tile], turned[tile])
        else:
            mixed = jnp.where(lane < 64, turned[tile], turned[tile + 1])
            mixed = jnp.where(lane < off - 80, left[tile + 1], mixed)
            mixed = jnp.where(lane >= off, left[tile], mixed)
        rows.append(roll_lanes(mixed, -off))
    return rows


def to_tiles(rows):
    lane = lane_index()
    turned_lane = jnp.where(lane < 64, lane + 64, lane - 64)
    placed = [roll_lanes(rows[y], 48 * y % 128) for y in range(8)]
    left, right = [], []
    for tile in range(3):
        a = c = None
        for y in range(8):
            lo, hi = max(48 * y, tile * 128), min(48 * y + 48, tile * 128 + 128)
            if lo >= hi:
                continue
            if a is None:
                a = c = placed[y]
            else:
                a = jnp.where(lane < lo - tile * 128, a, placed[y])
                c = jnp.where(turned_lane < lo - tile * 128, c, placed[y])
        left.append(a)
        right.append(roll_lanes(c, 64))
    return left, right


def three_terms(v):
    parts = []
    for _ in range(3):
        part = v.astype(BF16).astype(F32)
        parts.append(part)
        v = v - part
    return parts


def invert_factor(r, out):
    lane = lax.broadcasted_iota(jnp.int32, (8, 128), 1)
    sub = lax.broadcasted_iota(jnp.int32, (8, 128), 0)
    splat = lambda v, i, j: jnp.broadcast_to(v[i:i + 1, j:j + 1], (8, 128))
    spread = lambda v, i: jnp.broadcast_to(v[i:i + 1], (8, 128))

    def body(first_row, k):
        rows = pl.ds(pl.multiple_of(8 * k, 8), 8)
        top = [r[rows, 0:128], r[rows, 128:256]]
        off = 8 * lax.rem(k, 16)
        block = pltpu.roll(jnp.where(k >= 16, top[1], top[0]), lax.rem(128 - off, 128), 1)
        s = {(i, j): splat(block, j, i) for i in range(8) for j in range(i + 1)}
        recip, low = [], {}
        for col in range(8):
            recip.append(1.0 / s[col, col])
            for i in range(col + 1, 8):
                low[i, col] = s[i, col] * recip[col]
            for i in range(col + 1, 8):
                for j in range(col + 1, i + 1):
                    s[i, j] = s[i, j] - low[i, col] * s[j, col]
        inv = {}
        for j in range(8):
            for i in range(j + 1, 8):
                t = low[i, j]
                for p in range(j + 1, i):
                    t = t + low[i, p] * inv[p, j]
                inv[i, j] = -t
        cols, cols_t = [], []
        for j in range(8):
            v = jnp.where(sub == j, 1.0, 0.0)
            for i in range(j + 1, 8):
                v = jnp.where(sub == i, inv[i, j], v)
            cols.append(v)
            w = jnp.where(sub == j, 1.0, 0.0)
            for i in range(j):
                w = jnp.where(sub == i, inv[j, i], w)
            cols_t.append(w)
        pivot = recip[0]
        for i in range(1, 8):
            pivot = jnp.where(sub == i, recip[i], pivot)
        zs, ss = [], []
        for t in range(2):
            local = lane + 128 * t - 8 * k
            inside = jnp.logical_and(local >= 0, local < 8)
            v = jnp.where(inside, jnp.where(local == sub, 1.0, 0.0), top[t])
            y = cols[0] * spread(v, 0)
            for j in range(1, 8):
                y = y + cols[j] * spread(v, j)
            out[rows, 128 * t:128 * t + 128] = jnp.where(local < 8, y * jnp.sqrt(pivot), 0.0)
            y = y * pivot
            z = cols_t[0] * spread(y, 0)
            for j in range(1, 8):
                z = z + cols_t[j] * spread(y, j)
            zs.append(z)
            ss.append(jnp.where(local < 8, 0.0, top[t]))
        z, w = three_terms(jnp.concatenate(zs, 1)), three_terms(jnp.concatenate(ss, 1))
        left = jnp.concatenate([w[0], w[0], w[1], w[0], w[1], w[2]], 0).astype(BF16)
        right = jnp.concatenate([z[0], z[1], z[0], z[2], z[1], z[0]], 0).astype(BF16)
        live = slice(8 * first_row, M)
        update = lax.dot_general(left[:, live], right, (((0,), (0,)), ((), ())),
                                 preferred_element_type=F32)
        local = lax.broadcasted_iota(jnp.int32, (M - 8 * first_row, 256), 1) - 8 * k
        inside = jnp.logical_and(local >= 0, local < 8)
        r[live, :] = jnp.where(inside, 0.0, r[live, :]) - update

    for part in range(3):
        def segment(k, c):
            body(8 * part, k)
            return c
        lax.fori_loop(8 * part, 8 * part + 8, segment, 0)


def kernel(x_ref, p_ref, w_hbm, c_hbm, out_ref, recv, pot_in, w_ref, c_ref, field_a, field_b, pot, pack,
           own, part, rs_buf, xy_buf, sums, gsum, packed, work, inv_ref, rot, gathered, send_sems, recv_sems, ready):
    b = lax.axis_index("band")
    d = lax.axis_index("dom")
    core = lax.rem(b, 2)
    y_pos, zh, x_pos = d // 8, lax.rem(d // 4, 2), lax.rem(d, 4)
    two = lax.rem(core + d, 2) == 0
    first = 3 * (d // 2) + lax.rem(d, 2) * (2 - core)
    me = d * 4 + b
    partner = b + 1 - 2 * core

    def remote(src, dst, send, receive, to_b, to_d):
        pltpu.make_async_remote_copy(
            src_ref=src, dst_ref=dst, send_sem=send_sems.at[send], recv_sem=recv_sems.at[receive],
            device_id=(to_b, to_d), device_id_type=MESH).start()

    def local(src, dst, receive):
        pltpu.make_async_copy(src, dst, recv_sems.at[receive]).start()

    def arrived(ref, receive):
        pltpu.make_async_copy(ref, ref, recv_sems.at[receive]).wait()

    def drain(ref, sem, times):
        def body(i, c):
            pltpu.make_async_copy(ref, ref, sem).wait()
            return c
        lax.fori_loop(0, times, body, 0)

    barrier = pltpu.get_barrier_semaphore()

    def greet(i, c):
        pl.semaphore_signal(barrier, inc=1, device_id=(b, lax.rem(d + i, 32)), device_id_type=MESH)
        return c

    def greet_again(i, c):
        pl.semaphore_signal(ready, inc=1, device_id=(b, lax.rem(d + i, 32)), device_id_type=MESH)
        return c

    lax.fori_loop(1, 32, greet, 0)
    for i in range(1, 4):
        pl.semaphore_signal(barrier, inc=1, device_id=(lax.rem(b + i, 4), d), device_id_type=MESH)
    pl.semaphore_wait(barrier, 34)

    half = p_ref.at[:, pl.ds(pl.multiple_of(1152 * core, 128), 1152)]
    half_dst = pot_in.at[core, lax.rem(d, 4), :, d // 4, :]

    def send_potential(i, c):
        remote(half, half_dst, 1, 2, b, lax.rem(d + i, 32))
        return c

    def send_orbital(slot):
        def send(i, c):
            to = lax.rem(d + i, 32)
            to_two = lax.rem(core + to, 2) == 0
            o = 3 * (to // 2) + lax.rem(to, 2) * (2 - core) + slot
            src = x_ref.at[:, o, :]
            dst = recv.at[slot, lax.rem(d, 4), :, d // 4, :]

            def start():
                remote(src, dst, 0, slot, b, to)

            if slot == 0:
                start()
            else:
                pl.when(to_two)(start)
            return c

        def keep():
            local(x_ref.at[:, first + slot, :], recv.at[slot, lax.rem(d, 4), :, d // 4, :], slot)

        if slot == 0:
            keep()
        else:
            pl.when(two)(keep)
        lax.fori_loop(1, 32, send, 0)

    send_orbital(0)
    local(half, half_dst, 2)
    lax.fori_loop(1, 32, send_potential, 0)
    lax.fori_loop(1, 32, greet_again, 0)
    local(w_hbm, w_ref, 12)
    local(c_hbm, c_ref, 13)
    pot[...] = jnp.full(pot.shape, DIAGONAL, F32)

    def unpack(load, store):
        def body(q, c):
            for yb in range(3):
                for j in range(3):
                    rows = to_rows(load(0, yb, q, j), load(1, yb, q, j))
                    for y in range(8):
                        store(yb * 8 + y, pl.ds(pl.multiple_of(q * 24 + 8 * j, 8), 8), rows[y])
            return c

        lax.fori_loop(0, 4, body, 0)

    def chunk(start, t):
        return pl.ds(start + 128 * t, 128)

    def load_potential(side, yb, q, j):
        return [pot_in[side, q, j, :, chunk(yb * 384, t)] for t in range(3)]

    def put(field, y, rows, v):
        field[y, rows, :] = v
        if y < 6 or y >= 18:
            field[24 + y, rows, :] = pltpu.roll(v, 64, 1)

    def store_potential(y, rows, v):
        v = SCALE * v
        pot[y, rows, :] = v + DIAGONAL
        put(field_b, y, rows, field_b[y, rows, :] + (0.5 * v) * field_a[y, rows, :])

    def step(src, dst, weight):
        def block(n):
            y0 = n * ROWS
            values = src[pl.ds(y0, ROWS)].reshape(ROWS * 96, 128)
            high = values.astype(BF16)
            low = (values - high.astype(F32)).astype(BF16)
            along_z = jnp.dot(jnp.concatenate([high, low], 1), w_ref[...], preferred_element_type=F32)
            along_x = []
            for r in range(0, ROWS, 2):
                one, other = slice(96 * r, 96 * r + 96), slice(96 * r + 96, 96 * r + 192)
                columns = jnp.concatenate([jnp.concatenate([high[one], high[other]], 1),
                                           jnp.concatenate([low[one], low[other]], 1)], 0)
                along_x.append(jnp.dot(c_ref[...], columns, preferred_element_type=F32))
            at = [(y0 + s) % 48 for s in range(-6, ROWS + 6)]
            for i in range(12):
                rows = pl.ds(8 * i, 8)
                near = [src[y, rows, :] for y in at]
                for r in range(ROWS):
                    acc = near[6 + r] * pot[y0 + r, rows, :]
                    for k in range(1, 7):
                        acc = acc + COEFS[k] * (near[6 + r + k] + near[6 + r - k])
                    z = along_z[96 * r + 8 * i:96 * r + 8 * i + 8]
                    half_lanes = slice(128 * (r % 2), 128 * (r % 2) + 128)
                    x = (along_x[r // 2][8 * i:8 * i + 8, half_lanes]
                         + along_x[r // 2][96 + 8 * i:96 + 8 * i + 8, half_lanes])
                    acc = acc + ((z[:, :128] + z[:, 128:]) + x)
                    put(dst, y0 + r, rows, weight * acc - dst[y0 + r, rows, :])

        for n in range(24 // ROWS):
            block(n)

    def quarter(band):
        return 14 * band - jnp.maximum(band - 1, 0)

    def spread(slot):
        def share(to_b, to_d):
            begin = 14 * to_b - max(to_b - 1, 0)
            return (pack.at[slot, lax.rem(to_d, 4), pl.ds(begin, TILES), to_d // 4, :],
                    own.at[:, 48 * b + first + slot, :])

        def send(i, c):
            to_d = lax.rem(d + i, 32)
            for to_b in range(4):
                src, dst = share(to_b, to_d)
                remote(src, dst, 2, 3, to_b, to_d)
            return c

        lax.fori_loop(1, 32, send, 0)
        for to_b in range(4):
            src, dst = share(to_b, d)

            @pl.when(to_b == b)
            def _():
                local(src, dst, 3)

            @pl.when(to_b != b)
            def _():
                remote(src, dst, 2, 3, to_b, d)

    def add_potential():
        arrived(pot_in.at[core], 2)
        remote(pot_in.at[core], pot_in.at[core], 7, 11, partner, d)
        arrived(pot_in.at[core], 11)
        unpack(load_potential, store_potential)

    def send_second():
        send_orbital(1)

    def filter_orbital(slot, c):
        def load(side, yb, q, j):
            return [recv[slot, q, j, :, chunk(yb * 384 + 1152 * side, t)] for t in range(3)]

        def store(y, rows, v):
            put(field_a, y, rows, v)
            field_b[y, rows, :] = jnp.zeros_like(v)

        def repack(q, c):
            for yb in range(3):
                for j in range(3):
                    rows = [field_a[yb * 8 + y, pl.ds(pl.multiple_of(q * 24 + 8 * j, 8), 8), :] for y in range(8)]
                    left, right = to_tiles(rows)
                    for t in range(3):
                        pack[slot, q, j * 18 + yb * 3 + t] = left[t]
                        pack[slot, q, j * 18 + 9 + yb * 3 + t] = right[t]
            return c

        arrived(recv.at[slot], slot)
        pl.when(slot == 0)(send_second)
        unpack(load, store)

        def steps(t, c):
            step(field_a, field_b, jnp.where(t == 0, 0.5, 1.0))
            pl.when(jnp.logical_and(slot == 0, t == 0))(add_potential)
            step(field_b, field_a, 1.0)
            return c

        lax.fori_loop(0, 2, steps, 0)

        @pl.when(slot == 0)
        def _():
            pl.semaphore_wait(ready, 31)

        lax.fori_loop(0, 4, repack, 0)
        spread(slot)
        return c

    arrived(w_ref, 12)
    arrived(c_ref, 13)
    lax.fori_loop(0, jnp.where(two, 2, 1), filter_orbital, 0)
    arrived(own, 3)

    z_peer = lax.rem(b + 2, 4)
    other = lax.rem(partner + 2, 4)
    PART = EARLY // 2

    def exchange(i):
        tiles = pl.ds(PART * i, PART)
        remote(own.at[tiles], gathered.at[1, tiles], 9, 14 + i, z_peer, d)

    def forward(i):
        tiles = pl.ds(PART * i, PART)
        arrived(gathered.at[1, tiles], 14 + i)
        remote(gathered.at[1, tiles], gathered.at[2, tiles], 11, 17 + i, partner, d)

    total = jnp.zeros((M, M), F32)
    for i in range(0, TILES, 2):
        one = own[i]
        if i == 0:
            one = jnp.where(b >= 2, 0.0, one)
        both = jnp.concatenate([one, own[i + 1]], 1)
        total = total + lax.dot_general(both, both, (((1,), (1,)), ((), ())), precision=lax.Precision.HIGHEST,
                                        preferred_element_type=F32)
    near = total[:, :128]
    far = jnp.concatenate([total[:, 128:], jnp.zeros((M, 64), F32)], 1)
    left_half = lax.broadcasted_iota(jnp.int32, (64, 128), 1) < 64
    packed[0:64] = near[0:64]
    packed[64:128] = jnp.where(left_half, far[0:64], near[64:128])
    packed[128:192] = jnp.where(left_half, far[64:128], pltpu.roll(far[128:192], 64, 1))
    for i in range(8):
        part[i] = packed[24 * i:24 * i + 24]

    mine = zh * 4 + b
    for i in range(1, 8):
        to = lax.rem(mine + i, 8)
        remote(part.at[to], rs_buf.at[mine], 4, 4, lax.rem(to, 4), y_pos * 8 + (to // 4) * 4 + x_pos)
    rs_buf[mine] = part[mine]
    arrived(rs_buf.at[pl.ds(0, 7)], 4)
    exchange(0)
    acc = rs_buf[0]
    for i in range(1, 8):
        acc = acc + rs_buf[i]
    sums[...] = acc
    spot = y_pos * 4 + x_pos
    for i in range(1, 16):
        to = lax.rem(spot + i, 16)
        remote(sums, xy_buf.at[spot], 5, 5, b, (to // 4) * 8 + zh * 4 + lax.rem(to, 4))
    xy_buf[spot] = acc
    arrived(xy_buf.at[pl.ds(0, 15)], 5)
    acc = xy_buf[0]
    for i in range(1, 16):
        acc = acc + xy_buf[i]
    acc = acc / CELLS
    gsum[mine] = acc
    for i in range(1, 8):
        to = lax.rem(mine + i, 8)
        remote(gsum.at[mine], gsum.at[mine], 6, 6, lax.rem(to, 4), y_pos * 8 + (to // 4) * 4 + x_pos)
    arrived(gsum.at[pl.ds(0, 7)], 6)

    exchange(1)
    remote(own.at[pl.ds(0, EARLY)], gathered.at[0, pl.ds(0, EARLY)], 10, 16, partner, d)
    for i in range(8):
        packed[24 * i:24 * i + 24] = gsum[i]
    work[0:64, 0:128] = packed[0:64]
    work[0:64, 128:256] = packed[64:128]
    work[64:128, 0:128] = packed[64:128]
    work[64:128, 128:256] = packed[128:192]
    work[128:192, 0:128] = packed[128:192]
    work[128:192, 128:256] = pltpu.roll(packed[128:192], 64, 1)
    invert_factor(work, inv_ref)

    def place(tile):
        return tile // 18, pl.ds(pl.multiple_of(128 * lax.rem(tile, 18), 128), 128)

    def product(rows, block, n):
        columns = jnp.concatenate([block[2 * n], block[2 * n + 1]], 1)
        return jnp.dot(rows, columns, precision=lax.Precision.HIGHEST, preferred_element_type=F32)

    def rotate(n, c):
        result = product(inv_ref[:, 0:M], own, EARLY // 2 + n)
        for i in range(2):
            plane, lanes = place(quarter(b) + EARLY + 2 * n + i)
            for band in range(4):
                rot[2 * n + i, band] = result[48 * band:48 * band + 48, 128 * i:128 * i + 128]
            for away in (2, 3, 1):
                to = lax.rem(b + away, 4)
                remote(rot.at[2 * n + i, to], out_ref.at[plane, :, lanes], 8, 7 + b, to, d)
            local(rot.at[2 * n + i, b], out_ref.at[plane, :, lanes], 7 + b)
        return c

    def rotate_early(block, band):
        def body(n, c):
            result = product(inv_ref[pl.ds(pl.multiple_of(48 * b, 8), 48), 0:M], block, n)
            for i in range(2):
                plane, lanes = place(quarter(band) + 2 * n + i)

                def keep():
                    out_ref[plane, :, lanes] = result[:, 128 * i:128 * i + 128]

                if i == 0:
                    pl.when(jnp.logical_or(band < 2, n > 0))(keep)
                else:
                    keep()
            return c

        lax.fori_loop(0, EARLY // 2, body, 0)

    lax.fori_loop(0, (TILES - EARLY) // 2, rotate, 0)
    forward(0)
    forward(1)
    rotate_early(own, b)
    arrived(gathered.at[0, pl.ds(0, EARLY)], 16)
    rotate_early(gathered.at[0], partner)
    rotate_early(gathered.at[1], z_peer)
    for i in range(2):
        arrived(gathered.at[2, pl.ds(PART * i, PART)], 17 + i)
    rotate_early(gathered.at[2], other)

    late = TILES - EARLY
    for band in range(4):
        arrived(rot.at[pl.ds(0, late), 0], 7 + band)
    drain(rot.at[0, 0], send_sems.at[8], 3 * late)
    drain(gathered.at[0, pl.ds(0, PART)], send_sems.at[9], 2)
    drain(gathered.at[0, pl.ds(0, EARLY)], send_sems.at[10], 1)
    drain(gathered.at[0, pl.ds(0, PART)], send_sems.at[11], 2)
    orbital = recv.at[0, 0, :, 0, :]
    drain(orbital, send_sems.at[0], jnp.where(two, 46, 47))
    drain(half_dst, send_sems.at[1], 31)
    drain(pot_in.at[0], send_sems.at[7], 1)
    share = pack.at[0, 0, pl.ds(0, TILES), 0, :]
    drain(share, send_sems.at[2], jnp.where(two, 254, 127))
    drain(sums, send_sems.at[4], 7)
    drain(sums, send_sems.at[5], 15)
    drain(sums, send_sems.at[6], 7)


def per_device(orbitals, potential):
    anywhere = pl.BlockSpec(memory_space=pl.ANY)
    out = pl.pallas_call(
        kernel,
        out_shape=jax.ShapeDtypeStruct((3, 48, 2304), F32),
        in_specs=[anywhere] * 4,
        out_specs=pl.BlockSpec(memory_space=pltpu.VMEM),
        scratch_shapes=[
            pltpu.VMEM((2, 4, 3, 8, 2304), F32),
            pltpu.VMEM((2, 4, 3, 8, 1152), F32),
            pltpu.VMEM((256, 256), BF16),
            pltpu.VMEM((192, 192), BF16),
            pltpu.VMEM((48, 96, 128), F32),
            pltpu.VMEM((48, 96, 128), F32),
            pltpu.VMEM((24, 96, 128), F32),
            pltpu.VMEM((2, 4, 54, 8, 128), F32),
            pltpu.VMEM((TILES, M, 128), F32),
            pltpu.VMEM((8, 24, 128), F32),
            pltpu.VMEM((8, 24, 128), F32),
            pltpu.VMEM((16, 24, 128), F32),
            pltpu.VMEM((24, 128), F32),
            pltpu.VMEM((8, 24, 128), F32),
            pltpu.VMEM((M, 128), F32),
            pltpu.VMEM((M, 256), F32),
            pltpu.VMEM((M, 256), F32),
            pltpu.VMEM((TILES - EARLY, 4, 48, 128), F32),
            pltpu.VMEM((3, EARLY, M, 128), F32),
            pltpu.SemaphoreType.DMA((12,)),
            pltpu.SemaphoreType.DMA((20,)),
            pltpu.SemaphoreType.REGULAR,
        ],
        compiler_params=pltpu.CompilerParams(
            collective_id=0, has_side_effects=True, vmem_limit_bytes=56 * 2**20),
    )(jnp.transpose(orbitals, (1, 0, 2)), potential, jnp.asarray(z_matrix()), jnp.asarray(x_matrix()))
    return jnp.transpose(out, (1, 0, 2))


def solution(mesh):
    placed = (P("band", "dom", None), P("dom", None))
    return jax.shard_map(
        per_device, mesh=mesh, in_specs=placed, out_specs=P("band", "dom", None), check_vma=False
    )
```

```python
import jax
import jax.numpy as jnp
import numpy as np
from jax import lax
from jax.experimental import pallas as pl
from jax.experimental.pallas import tpu as pltpu
from jax.sharding import PartitionSpec as P

M = 192
CELLS = 221184
MESH = pl.DeviceIdType.MESH
F32, BF16 = jnp.float32, jnp.bfloat16

stencil_weights = (
    -5369.0 / 1800.0,
    12.0 / 7.0,
    -15.0 / 56.0,
    10.0 / 189.0,
    -1.0 / 112.0,
    2.0 / 1925.0,
    -1.0 / 16632.0,
)
SCALE = 0.4
COEFS = [-0.5 * SCALE * w for w in stencil_weights]
DIAGONAL = 3.0 * COEFS[0] - 7.0 * SCALE
TILES = 14
EARLY = 6
ROWS = 8


def two_terms(full):
    high = full.astype(BF16)
    return high, (full - high.astype(np.float32)).astype(BF16)


def z_matrix():
    full = np.zeros((128, 128), np.float32)
    for half in range(2):
        for z in range(48):
            for k in range(1, 7):
                full[half * 64 + z, half * 64 + (z + k) % 48] += COEFS[k]
                full[half * 64 + z, half * 64 + (z - k) % 48] += COEFS[k]
    row = np.concatenate(two_terms(full), 1)
    return np.concatenate([row, row], 0)


def x_matrix():
    full = np.zeros((96, 96), np.float32)
    place = [(r % 8) * 12 + r // 8 for r in range(96)]
    for a in range(96):
        for c in range(96):
            away = (place[a] - place[c]) % 96
            away = min(away, 96 - away)
            if 1 <= away <= 6:
                full[a, c] = COEFS[away]
    high, low = two_terms(full)
    return np.concatenate([np.concatenate([high, high], 1), np.concatenate([low, low], 1)], 0)


def roll_lanes(v, by):
    by = by % 128
    return v if by == 0 else pltpu.roll(v, by, 1)


def lane_index():
    return lax.broadcasted_iota(jnp.int32, (8, 128), 1)


def to_rows(left, right):
    lane = lane_index()
    turned = [roll_lanes(v, 64) for v in right]
    rows = []
    for y in range(8):
        tile, off = 48 * y // 128, 48 * y % 128
        if off + 48 <= 128:
            inside = jnp.logical_and(lane >= off, lane < off + 48)
            mixed = jnp.where(inside, left[tile], turned[tile])
        else:
            mixed = jnp.where(lane < 64, turned[tile], turned[tile + 1])
            mixed = jnp.where(lane < off - 80, left[tile + 1], mixed)
            mixed = jnp.where(lane >= off, left[tile], mixed)
        rows.append(roll_lanes(mixed, -off))
    return rows


def to_tiles(rows):
    lane = lane_index()
    turned_lane = jnp.where(lane < 64, lane + 64, lane - 64)
    placed = [roll_lanes(rows[y], 48 * y % 128) for y in range(8)]
    left, right = [], []
    for tile in range(3):
        a = c = None
        for y in range(8):
            lo, hi = max(48 * y, tile * 128), min(48 * y + 48, tile * 128 + 128)
            if lo >= hi:
                continue
            if a is None:
                a = c = placed[y]
            else:
                a = jnp.where(lane < lo - tile * 128, a, placed[y])
                c = jnp.where(turned_lane < lo - tile * 128, c, placed[y])
        left.append(a)
        right.append(roll_lanes(c, 64))
    return left, right


def three_terms(v):
    parts = []
    for _ in range(3):
        part = v.astype(BF16).astype(F32)
        parts.append(part)
        v = v - part
    return parts


def invert_factor(r, out, wide):
    lane = lax.broadcasted_iota(jnp.int32, (8, 128), 1)
    sub = lax.broadcasted_iota(jnp.int32, (8, 128), 0)
    spread = lambda v, i: jnp.broadcast_to(v[i:i + 1], (8, 128))

    def body(first_row, k):
        rows = pl.ds(8 * k, 8)
        top = [r[rows, 0:128], r[rows, 128:256]]
        base = 64 * (k % 2)
        for i in range(8):
            at = 8 * (k % 16) + i
            wide[base + 8 * i:base + 8 * i + 8, :] = jnp.broadcast_to(top[k // 16][:, at:at + 1], (8, 128))
        s = {(i, j): jnp.broadcast_to(wide[base + 8 * i + j:base + 8 * i + j + 1, :], (8, 128))
             for i in range(8) for j in range(i + 1)}
        recip, low = [], {}
        for col in range(8):
            recip.append(1.0 / s[col, col])
            for i in range(col + 1, 8):
                low[i, col] = s[i, col] * recip[col]
            for i in range(col + 1, 8):
                for j in range(col + 1, i + 1):
                    s[i, j] = s[i, j] - low[i, col] * s[j, col]
        inv = {}
        for j in range(8):
            for i in range(j + 1, 8):
                t = low[i, j]
                for p in range(j + 1, i):
                    t = t + low[i, p] * inv[p, j]
                inv[i, j] = -t
        cols, cols_t = [], []
        for j in range(8):
            v = jnp.where(sub == j, 1.0, 0.0)
            for i in range(j + 1, 8):
                v = jnp.where(sub == i, inv[i, j], v)
            cols.append(v)
            w = jnp.where(sub == j, 1.0, 0.0)
            for i in range(j):
                w = jnp.where(sub == i, inv[j, i], w)
            cols_t.append(w)
        pivot = recip[0]
        for i in range(1, 8):
            pivot = jnp.where(sub == i, recip[i], pivot)
        zs, ss = [], []
        for t in range(2):
            local = lane + 128 * t - 8 * k
            inside = jnp.logical_and(local >= 0, local < 8)
            v = jnp.where(inside, jnp.where(local == sub, 1.0, 0.0), top[t])
            y = cols[0] * spread(v, 0)
            for j in range(1, 8):
                y = y + cols[j] * spread(v, j)
            out[rows, 128 * t:128 * t + 128] = jnp.where(local < 8, y * jnp.sqrt(pivot), 0.0)
            y = y * pivot
            z = cols_t[0] * spread(y, 0)
            for j in range(1, 8):
                z = z + cols_t[j] * spread(y, j)
            zs.append(z)
            ss.append(jnp.where(local < 8, 0.0, top[t]))
        z, w = three_terms(jnp.concatenate(zs, 1)), three_terms(jnp.concatenate(ss, 1))
        left = jnp.concatenate([w[0], w[0], w[1], w[0], w[1], w[2]], 0).astype(BF16)
        right = jnp.concatenate([z[0], z[1], z[0], z[2], z[1], z[0]], 0).astype(BF16)
        if first_row == 24:
            return
        live = slice(8 * first_row, M)
        update = lax.dot_general(left[:, live], right, (((0,), (0,)), ((), ())),
                                 preferred_element_type=F32)
        local = lax.broadcasted_iota(jnp.int32, (M - 8 * first_row, 256), 1) - 8 * k
        inside = jnp.logical_and(local >= 0, local < 8)
        r[live, :] = jnp.where(inside, 0.0, r[live, :]) - update

    for k in range(24):
        body(k + 1, k)


def kernel(x_ref, p_ref, w_hbm, c_hbm, out_ref, recv, pot_in, w_ref, c_ref, field_a, field_b, pot, pack,
           own, part, rs_buf, xy_buf, sums, gsum, packed, work, inv_ref, wide, rot, gathered, send_sems, recv_sems, ready):
    b = lax.axis_index("band")
    d = lax.axis_index("dom")
    core = lax.rem(b, 2)
    y_pos, zh, x_pos = d // 8, lax.rem(d // 4, 2), lax.rem(d, 4)
    two = lax.rem(core + d, 2) == 0
    first = 3 * (d // 2) + lax.rem(d, 2) * (2 - core)
    me = d * 4 + b
    partner = b + 1 - 2 * core

    def remote(src, dst, send, receive, to_b, to_d):
        pltpu.make_async_remote_copy(
            src_ref=src, dst_ref=dst, send_sem=send_sems.at[send], recv_sem=recv_sems.at[receive],
            device_id=(to_b, to_d), device_id_type=MESH).start()

    def local(src, dst, receive):
        pltpu.make_async_copy(src, dst, recv_sems.at[receive]).start()

    def arrived(ref, receive):
        pltpu.make_async_copy(ref, ref, recv_sems.at[receive]).wait()

    def drain(ref, sem, times):
        def body(i, c):
            pltpu.make_async_copy(ref, ref, sem).wait()
            return c
        lax.fori_loop(0, times, body, 0)

    barrier = pltpu.get_barrier_semaphore()

    def greet(i, c):
        pl.semaphore_signal(barrier, inc=1, device_id=(b, lax.rem(d + i, 32)), device_id_type=MESH)
        return c

    def greet_again(i, c):
        pl.semaphore_signal(ready, inc=1, device_id=(b, lax.rem(d + i, 32)), device_id_type=MESH)
        return c

    lax.fori_loop(1, 32, greet, 0)
    for i in range(1, 4):
        pl.semaphore_signal(barrier, inc=1, device_id=(lax.rem(b + i, 4), d), device_id_type=MESH)
    pl.semaphore_wait(barrier, 34)

    half = p_ref.at[:, pl.ds(pl.multiple_of(1152 * core, 128), 1152)]
    half_dst = pot_in.at[core, lax.rem(d, 4), :, d // 4, :]

    def send_potential(i, c):
        remote(half, half_dst, 1, 2, b, lax.rem(d + i, 32))
        return c

    def send_orbital(slot):
        def send(i, c):
            to = lax.rem(d + i, 32)
            to_two = lax.rem(core + to, 2) == 0
            o = 3 * (to // 2) + lax.rem(to, 2) * (2 - core) + slot
            src = x_ref.at[:, o, :]
            dst = recv.at[slot, lax.rem(d, 4), :, d // 4, :]

            def start():
                remote(src, dst, 0, slot, b, to)

            if slot == 0:
                start()
            else:
                pl.when(to_two)(start)
            return c

        def keep():
            local(x_ref.at[:, first + slot, :], recv.at[slot, lax.rem(d, 4), :, d // 4, :], slot)

        if slot == 0:
            keep()
        else:
            pl.when(two)(keep)
        lax.fori_loop(1, 32, send, 0)

    send_orbital(0)
    local(half, half_dst, 2)
    lax.fori_loop(1, 32, send_potential, 0)
    lax.fori_loop(1, 32, greet_again, 0)
    local(w_hbm, w_ref, 12)
    local(c_hbm, c_ref, 13)
    pot[...] = jnp.full(pot.shape, DIAGONAL, F32)

    def unpack(load, store):
        def body(q, c):
            for yb in range(3):
                for j in range(3):
                    rows = to_rows(load(0, yb, q, j), load(1, yb, q, j))
                    for y in range(8):
                        store(yb * 8 + y, pl.ds(pl.multiple_of(q * 24 + 8 * j, 8), 8), rows[y])
            return c

        lax.fori_loop(0, 4, body, 0)

    def chunk(start, t):
        return pl.ds(start + 128 * t, 128)

    def load_potential(side, yb, q, j):
        return [pot_in[side, q, j, :, chunk(yb * 384, t)] for t in range(3)]

    def put(field, y, rows, v):
        field[y, rows, :] = v
        if y < 6 or y >= 18:
            field[24 + y, rows, :] = pltpu.roll(v, 64, 1)

    def store_potential(y, rows, v):
        v = SCALE * v
        pot[y, rows, :] = v + DIAGONAL
        put(field_b, y, rows, field_b[y, rows, :] + (0.5 * v) * field_a[y, rows, :])

    def step(src, dst, weight):
        def block(n):
            y0 = n * ROWS
            values = src[pl.ds(y0, ROWS)].reshape(ROWS * 96, 128)
            high = values.astype(BF16)
            low = (values - high.astype(F32)).astype(BF16)
            along_z = jnp.dot(jnp.concatenate([high, low], 1), w_ref[...], preferred_element_type=F32)
            along_x = []
            for r in range(0, ROWS, 2):
                one, other = slice(96 * r, 96 * r + 96), slice(96 * r + 96, 96 * r + 192)
                columns = jnp.concatenate([jnp.concatenate([high[one], high[other]], 1),
                                           jnp.concatenate([low[one], low[other]], 1)], 0)
                along_x.append(jnp.dot(c_ref[...], columns, preferred_element_type=F32))
            at = [(y0 + s) % 48 for s in range(-6, ROWS + 6)]
            for i in range(12):
                rows = pl.ds(8 * i, 8)
                near = [src[y, rows, :] for y in at]
                for r in range(ROWS):
                    acc = near[6 + r] * pot[y0 + r, rows, :]
                    for k in range(1, 7):
                        acc = acc + COEFS[k] * (near[6 + r + k] + near[6 + r - k])
                    z = along_z[96 * r + 8 * i:96 * r + 8 * i + 8]
                    half_lanes = slice(128 * (r % 2), 128 * (r % 2) + 128)
                    x = (along_x[r // 2][8 * i:8 * i + 8, half_lanes]
                         + along_x[r // 2][96 + 8 * i:96 + 8 * i + 8, half_lanes])
                    acc = acc + ((z[:, :128] + z[:, 128:]) + x)
                    put(dst, y0 + r, rows, weight * acc - dst[y0 + r, rows, :])

        for n in range(24 // ROWS):
            block(n)

    def quarter(band):
        return 14 * band - jnp.maximum(band - 1, 0)

    def spread(slot):
        def share(to_b, to_d):
            begin = 14 * to_b - max(to_b - 1, 0)
            return (pack.at[slot, lax.rem(to_d, 4), pl.ds(begin, TILES), to_d // 4, :],
                    own.at[:, 48 * b + first + slot, :])

        def send(i, c):
            to_d = lax.rem(d + i, 32)
            for to_b in range(4):
                src, dst = share(to_b, to_d)
                remote(src, dst, 2, 3, to_b, to_d)
            return c

        lax.fori_loop(1, 32, send, 0)
        for to_b in range(4):
            src, dst = share(to_b, d)

            @pl.when(to_b == b)
            def _():
                local(src, dst, 3)

            @pl.when(to_b != b)
            def _():
                remote(src, dst, 2, 3, to_b, d)

    def add_potential():
        arrived(pot_in.at[core], 2)
        remote(pot_in.at[core], pot_in.at[core], 7, 11, partner, d)
        arrived(pot_in.at[core], 11)
        unpack(load_potential, store_potential)

    def send_second():
        send_orbital(1)

    def filter_orbital(slot, c):
        def load(side, yb, q, j):
            return [recv[slot, q, j, :, chunk(yb * 384 + 1152 * side, t)] for t in range(3)]

        def store(y, rows, v):
            put(field_a, y, rows, v)
            field_b[y, rows, :] = jnp.zeros_like(v)

        def repack(q, c):
            for yb in range(3):
                for j in range(3):
                    rows = [field_a[yb * 8 + y, pl.ds(pl.multiple_of(q * 24 + 8 * j, 8), 8), :] for y in range(8)]
                    left, right = to_tiles(rows)
                    for t in range(3):
                        pack[slot, q, j * 18 + yb * 3 + t] = left[t]
                        pack[slot, q, j * 18 + 9 + yb * 3 + t] = right[t]
            return c

        arrived(recv.at[slot], slot)
        pl.when(slot == 0)(send_second)
        unpack(load, store)

        def steps(t, c):
            step(field_a, field_b, jnp.where(t == 0, 0.5, 1.0))
            pl.when(jnp.logical_and(slot == 0, t == 0))(add_potential)
            step(field_b, field_a, 1.0)
            return c

        lax.fori_loop(0, 2, steps, 0)

        @pl.when(slot == 0)
        def _():
            pl.semaphore_wait(ready, 31)

        lax.fori_loop(0, 4, repack, 0)
        spread(slot)
        return c

    arrived(w_ref, 12)
    arrived(c_ref, 13)
    lax.fori_loop(0, jnp.where(two, 2, 1), filter_orbital, 0)
    arrived(own, 3)

    z_peer = lax.rem(b + 2, 4)
    other = lax.rem(partner + 2, 4)
    PART = EARLY // 2

    def exchange(i):
        tiles = pl.ds(PART * i, PART)
        remote(own.at[tiles], gathered.at[1, tiles], 9, 14 + i, z_peer, d)

    def forward(i):
        tiles = pl.ds(PART * i, PART)
        arrived(gathered.at[1, tiles], 14 + i)
        remote(gathered.at[1, tiles], gathered.at[2, tiles], 11, 17 + i, partner, d)

    total = jnp.zeros((M, M), F32)
    for i in range(0, TILES, 2):
        one = own[i]
        if i == 0:
            one = jnp.where(b >= 2, 0.0, one)
        both = jnp.concatenate([one, own[i + 1]], 1)
        total = total + lax.dot_general(both, both, (((1,), (1,)), ((), ())), precision=lax.Precision.HIGHEST,
                                        preferred_element_type=F32)
    near = total[:, :128]
    far = jnp.concatenate([total[:, 128:], jnp.zeros((M, 64), F32)], 1)
    left_half = lax.broadcasted_iota(jnp.int32, (64, 128), 1) < 64
    packed[0:64] = near[0:64]
    packed[64:128] = jnp.where(left_half, far[0:64], near[64:128])
    packed[128:192] = jnp.where(left_half, far[64:128], pltpu.roll(far[128:192], 64, 1))
    for i in range(8):
        part[i] = packed[24 * i:24 * i + 24]

    mine = zh * 4 + b
    for i in range(1, 8):
        to = lax.rem(mine + i, 8)
        remote(part.at[to], rs_buf.at[mine], 4, 4, lax.rem(to, 4), y_pos * 8 + (to // 4) * 4 + x_pos)
    rs_buf[mine] = part[mine]
    arrived(rs_buf.at[pl.ds(0, 7)], 4)
    exchange(0)
    acc = rs_buf[0]
    for i in range(1, 8):
        acc = acc + rs_buf[i]
    sums[...] = acc
    spot = y_pos * 4 + x_pos
    for i in range(1, 16):
        to = lax.rem(spot + i, 16)
        remote(sums, xy_buf.at[spot], 5, 5, b, (to // 4) * 8 + zh * 4 + lax.rem(to, 4))
    xy_buf[spot] = acc
    arrived(xy_buf.at[pl.ds(0, 15)], 5)
    acc = xy_buf[0]
    for i in range(1, 16):
        acc = acc + xy_buf[i]
    acc = acc / CELLS
    gsum[mine] = acc
    for i in range(1, 8):
        to = lax.rem(mine + i, 8)
        remote(gsum.at[mine], gsum.at[mine], 6, 6, lax.rem(to, 4), y_pos * 8 + (to // 4) * 4 + x_pos)
    arrived(gsum.at[pl.ds(0, 7)], 6)

    exchange(1)
    remote(own.at[pl.ds(0, EARLY)], gathered.at[0, pl.ds(0, EARLY)], 10, 16, partner, d)
    for i in range(8):
        packed[24 * i:24 * i + 24] = gsum[i]
    work[0:64, 0:128] = packed[0:64]
    work[0:64, 128:256] = packed[64:128]
    work[64:128, 0:128] = packed[64:128]
    work[64:128, 128:256] = packed[128:192]
    work[128:192, 0:128] = packed[128:192]
    work[128:192, 128:256] = pltpu.roll(packed[128:192], 64, 1)
    invert_factor(work, inv_ref, wide)

    def place(tile):
        return tile // 18, pl.ds(pl.multiple_of(128 * lax.rem(tile, 18), 128), 128)

    def product(rows, block, n):
        columns = jnp.concatenate([block[2 * n], block[2 * n + 1]], 1)
        return jnp.dot(rows, columns, precision=lax.Precision.HIGHEST, preferred_element_type=F32)

    def rotate(n, c):
        result = product(inv_ref[:, 0:M], own, EARLY // 2 + n)
        for i in range(2):
            plane, lanes = place(quarter(b) + EARLY + 2 * n + i)
            for band in range(4):
                rot[2 * n + i, band] = result[48 * band:48 * band + 48, 128 * i:128 * i + 128]
            for away in (2, 3, 1):
                to = lax.rem(b + away, 4)
                remote(rot.at[2 * n + i, to], out_ref.at[plane, :, lanes], 8, 7 + b, to, d)
            local(rot.at[2 * n + i, b], out_ref.at[plane, :, lanes], 7 + b)
        return c

    def rotate_early(block, band):
        def body(n, c):
            result = product(inv_ref[pl.ds(pl.multiple_of(48 * b, 8), 48), 0:M], block, n)
            for i in range(2):
                plane, lanes = place(quarter(band) + 2 * n + i)

                def keep():
                    out_ref[plane, :, lanes] = result[:, 128 * i:128 * i + 128]

                if i == 0:
                    pl.when(jnp.logical_or(band < 2, n > 0))(keep)
                else:
                    keep()
            return c

        lax.fori_loop(0, EARLY // 2, body, 0)

    lax.fori_loop(0, (TILES - EARLY) // 2, rotate, 0)
    forward(0)
    forward(1)
    rotate_early(own, b)
    arrived(gathered.at[0, pl.ds(0, EARLY)], 16)
    rotate_early(gathered.at[0], partner)
    rotate_early(gathered.at[1], z_peer)
    for i in range(2):
        arrived(gathered.at[2, pl.ds(PART * i, PART)], 17 + i)
    rotate_early(gathered.at[2], other)

    late = TILES - EARLY
    for band in range(4):
        arrived(rot.at[pl.ds(0, late), 0], 7 + band)
    drain(rot.at[0, 0], send_sems.at[8], 3 * late)
    drain(gathered.at[0, pl.ds(0, PART)], send_sems.at[9], 2)
    drain(gathered.at[0, pl.ds(0, EARLY)], send_sems.at[10], 1)
    drain(gathered.at[0, pl.ds(0, PART)], send_sems.at[11], 2)
    orbital = recv.at[0, 0, :, 0, :]
    drain(orbital, send_sems.at[0], jnp.where(two, 46, 47))
    drain(half_dst, send_sems.at[1], 31)
    drain(pot_in.at[0], send_sems.at[7], 1)
    share = pack.at[0, 0, pl.ds(0, TILES), 0, :]
    drain(share, send_sems.at[2], jnp.where(two, 254, 127))
    drain(sums, send_sems.at[4], 7)
    drain(sums, send_sems.at[5], 15)
    drain(sums, send_sems.at[6], 7)


def per_device(orbitals, potential):
    anywhere = pl.BlockSpec(memory_space=pl.ANY)
    out = pl.pallas_call(
        kernel,
        out_shape=jax.ShapeDtypeStruct((3, 48, 2304), F32),
        in_specs=[anywhere] * 4,
        out_specs=pl.BlockSpec(memory_space=pltpu.VMEM),
        scratch_shapes=[
            pltpu.VMEM((2, 4, 3, 8, 2304), F32),
            pltpu.VMEM((2, 4, 3, 8, 1152), F32),
            pltpu.VMEM((256, 256), BF16),
            pltpu.VMEM((192, 192), BF16),
            pltpu.VMEM((48, 96, 128), F32),
            pltpu.VMEM((48, 96, 128), F32),
            pltpu.VMEM((24, 96, 128), F32),
            pltpu.VMEM((2, 4, 54, 8, 128), F32),
            pltpu.VMEM((TILES, M, 128), F32),
            pltpu.VMEM((8, 24, 128), F32),
            pltpu.VMEM((8, 24, 128), F32),
            pltpu.VMEM((16, 24, 128), F32),
            pltpu.VMEM((24, 128), F32),
            pltpu.VMEM((8, 24, 128), F32),
            pltpu.VMEM((M, 128), F32),
            pltpu.VMEM((M, 256), F32),
            pltpu.VMEM((M, 256), F32),
            pltpu.VMEM((128, 128), F32),
            pltpu.VMEM((TILES - EARLY, 4, 48, 128), F32),
            pltpu.VMEM((3, EARLY, M, 128), F32),
            pltpu.SemaphoreType.DMA((12,)),
            pltpu.SemaphoreType.DMA((20,)),
            pltpu.SemaphoreType.REGULAR,
        ],
        compiler_params=pltpu.CompilerParams(
            collective_id=0, has_side_effects=True, vmem_limit_bytes=56 * 2**20),
    )(jnp.transpose(orbitals, (1, 0, 2)), potential, jnp.asarray(z_matrix()), jnp.asarray(x_matrix()))
    return jnp.transpose(out, (1, 0, 2))


def solution(mesh):
    placed = (P("band", "dom", None), P("dom", None))
    return jax.shard_map(
        per_device, mesh=mesh, in_specs=placed, out_specs=P("band", "dom", None), check_vma=False
    )
```

```python
import jax
import jax.numpy as jnp
import numpy as np
from jax import lax
from jax.experimental import pallas as pl
from jax.experimental.pallas import tpu as pltpu
from jax.sharding import PartitionSpec as P

M = 192
CELLS = 221184
MESH = pl.DeviceIdType.MESH
F32, BF16 = jnp.float32, jnp.bfloat16

stencil_weights = (
    -5369.0 / 1800.0,
    12.0 / 7.0,
    -15.0 / 56.0,
    10.0 / 189.0,
    -1.0 / 112.0,
    2.0 / 1925.0,
    -1.0 / 16632.0,
)
SCALE = 0.4
COEFS = [-0.5 * SCALE * w for w in stencil_weights]
DIAGONAL = 3.0 * COEFS[0] - 7.0 * SCALE
TILES = 14
EARLY = 6
ROWS = 8


def two_terms(full):
    high = full.astype(BF16)
    return high, (full - high.astype(np.float32)).astype(BF16)


def z_matrix():
    full = np.zeros((128, 128), np.float32)
    for half in range(2):
        for z in range(48):
            for k in range(1, 7):
                full[half * 64 + z, half * 64 + (z + k) % 48] += COEFS[k]
                full[half * 64 + z, half * 64 + (z - k) % 48] += COEFS[k]
    row = np.concatenate(two_terms(full), 1)
    return np.concatenate([row, row], 0)


def x_matrix():
    full = np.zeros((96, 96), np.float32)
    place = [(r % 8) * 12 + r // 8 for r in range(96)]
    for a in range(96):
        for c in range(96):
            away = (place[a] - place[c]) % 96
            away = min(away, 96 - away)
            if 1 <= away <= 6:
                full[a, c] = COEFS[away]
    high, low = two_terms(full)
    return np.concatenate([np.concatenate([high, high], 1), np.concatenate([low, low], 1)], 0)


def roll_lanes(v, by):
    by = by % 128
    return v if by == 0 else pltpu.roll(v, by, 1)


def lane_index():
    return lax.broadcasted_iota(jnp.int32, (8, 128), 1)


def to_rows(left, right):
    lane = lane_index()
    turned = [roll_lanes(v, 64) for v in right]
    rows = []
    for y in range(8):
        tile, off = 48 * y // 128, 48 * y % 128
        if off + 48 <= 128:
            inside = jnp.logical_and(lane >= off, lane < off + 48)
            mixed = jnp.where(inside, left[tile], turned[tile])
        else:
            mixed = jnp.where(lane < 64, turned[tile], turned[tile + 1])
            mixed = jnp.where(lane < off - 80, left[tile + 1], mixed)
            mixed = jnp.where(lane >= off, left[tile], mixed)
        rows.append(roll_lanes(mixed, -off))
    return rows


def to_tiles(rows):
    lane = lane_index()
    turned_lane = jnp.where(lane < 64, lane + 64, lane - 64)
    placed = [roll_lanes(rows[y], 48 * y % 128) for y in range(8)]
    left, right = [], []
    for tile in range(3):
        a = c = None
        for y in range(8):
            lo, hi = max(48 * y, tile * 128), min(48 * y + 48, tile * 128 + 128)
            if lo >= hi:
                continue
            if a is None:
                a = c = placed[y]
            else:
                a = jnp.where(lane < lo - tile * 128, a, placed[y])
                c = jnp.where(turned_lane < lo - tile * 128, c, placed[y])
        left.append(a)
        right.append(roll_lanes(c, 64))
    return left, right


def three_terms(v):
    parts = []
    for _ in range(3):
        part = v.astype(BF16).astype(F32)
        parts.append(part)
        v = v - part
    return parts


def invert_factor(r, out, wide):
    lane = lax.broadcasted_iota(jnp.int32, (8, 128), 1)
    sub = lax.broadcasted_iota(jnp.int32, (8, 128), 0)
    spread = lambda v, i: jnp.broadcast_to(v[i:i + 1], (8, 128))

    def body(first_row, k):
        rows = pl.ds(8 * k, 8)
        top = [r[rows, 0:128], r[rows, 128:256]]
        base = 64 * (k % 2)
        for i in range(8):
            at = 8 * (k % 16) + i
            wide[base + 8 * i:base + 8 * i + 8, :] = jnp.broadcast_to(top[k // 16][:, at:at + 1], (8, 128))
        s = {(i, j): jnp.broadcast_to(wide[base + 8 * i + j:base + 8 * i + j + 1, :], (8, 128))
             for i in range(8) for j in range(i + 1)}
        recip, low = [], {}
        for col in range(8):
            recip.append(1.0 / s[col, col])
            for i in range(col + 1, 8):
                low[i, col] = s[i, col] * recip[col]
            for i in range(col + 1, 8):
                for j in range(col + 1, i + 1):
                    s[i, j] = s[i, j] - low[i, col] * s[j, col]
        inv = {}
        for j in range(8):
            for i in range(j + 1, 8):
                t = low[i, j]
                for p in range(j + 1, i):
                    t = t + low[i, p] * inv[p, j]
                inv[i, j] = -t
        cols, cols_t = [], []
        for j in range(8):
            v = jnp.where(sub == j, 1.0, 0.0)
            for i in range(j + 1, 8):
                v = jnp.where(sub == i, inv[i, j], v)
            cols.append(v)
            w = jnp.where(sub == j, 1.0, 0.0)
            for i in range(j):
                w = jnp.where(sub == i, inv[j, i], w)
            cols_t.append(w)
        pivot = recip[0]
        for i in range(1, 8):
            pivot = jnp.where(sub == i, recip[i], pivot)
        zs, ss = [], []
        for t in range(2):
            local = lane + 128 * t - 8 * k
            inside = jnp.logical_and(local >= 0, local < 8)
            v = jnp.where(inside, jnp.where(local == sub, 1.0, 0.0), top[t])
            y = cols[0] * spread(v, 0)
            for j in range(1, 8):
                y = y + cols[j] * spread(v, j)
            out[rows, 128 * t:128 * t + 128] = jnp.where(local < 8, y * jnp.sqrt(pivot), 0.0)
            y = y * pivot
            z = cols_t[0] * spread(y, 0)
            for j in range(1, 8):
                z = z + cols_t[j] * spread(y, j)
            zs.append(z)
            ss.append(jnp.where(local < 8, 0.0, top[t]))
        z, w = three_terms(jnp.concatenate(zs, 1)), three_terms(jnp.concatenate(ss, 1))
        left = jnp.concatenate([w[0], w[0], w[1], w[0], w[1], w[2]], 0).astype(BF16)
        right = jnp.concatenate([z[0], z[1], z[0], z[2], z[1], z[0]], 0).astype(BF16)
        if first_row == 24:
            return
        live = slice(8 * first_row, M)
        update = lax.dot_general(left[:, live], right, (((0,), (0,)), ((), ())),
                                 preferred_element_type=F32)
        local = lax.broadcasted_iota(jnp.int32, (M - 8 * first_row, 256), 1) - 8 * k
        inside = jnp.logical_and(local >= 0, local < 8)
        r[live, :] = jnp.where(inside, 0.0, r[live, :]) - update

    for k in range(24):
        body(k + 1, k)


def kernel(x_ref, p_ref, w_hbm, c_hbm, out_ref, recv, pot_in, w_ref, c_ref, field_a, field_b, pot, pack,
           own, part, rs_buf, xy_buf, sums, gsum, packed, work, inv_ref, wide, rot, gathered, send_sems, recv_sems, ready):
    b = lax.axis_index("band")
    d = lax.axis_index("dom")
    core = lax.rem(b, 2)
    y_pos, zh, x_pos = d // 8, lax.rem(d // 4, 2), lax.rem(d, 4)
    two = lax.rem(core + d, 2) == 0
    first = 3 * (d // 2) + lax.rem(d, 2) * (2 - core)
    me = d * 4 + b
    partner = b + 1 - 2 * core

    def remote(src, dst, send, receive, to_b, to_d):
        pltpu.make_async_remote_copy(
            src_ref=src, dst_ref=dst, send_sem=send_sems.at[send], recv_sem=recv_sems.at[receive],
            device_id=(to_b, to_d), device_id_type=MESH).start()

    def local(src, dst, receive):
        pltpu.make_async_copy(src, dst, recv_sems.at[receive]).start()

    def arrived(ref, receive):
        pltpu.make_async_copy(ref, ref, recv_sems.at[receive]).wait()

    def drain(ref, sem, times):
        def body(i, c):
            pltpu.make_async_copy(ref, ref, sem).wait()
            return c
        lax.fori_loop(0, times, body, 0)

    barrier = pltpu.get_barrier_semaphore()

    def greet(i, c):
        pl.semaphore_signal(barrier, inc=1, device_id=(b, lax.rem(d + i, 32)), device_id_type=MESH)
        return c

    def greet_again(i, c):
        pl.semaphore_signal(ready, inc=1, device_id=(b, lax.rem(d + i, 32)), device_id_type=MESH)
        return c

    lax.fori_loop(1, 32, greet, 0)
    for i in range(1, 4):
        pl.semaphore_signal(barrier, inc=1, device_id=(lax.rem(b + i, 4), d), device_id_type=MESH)
    pl.semaphore_wait(barrier, 34)

    half = p_ref.at[:, pl.ds(pl.multiple_of(1152 * core, 128), 1152)]
    half_dst = pot_in.at[core, lax.rem(d, 4), :, d // 4, :]

    def send_potential(i, c):
        remote(half, half_dst, 1, 2, b, lax.rem(d + i, 32))
        return c

    def send_orbital(slot):
        def send(i, c):
            to = lax.rem(d + i, 32)
            to_two = lax.rem(core + to, 2) == 0
            o = 3 * (to // 2) + lax.rem(to, 2) * (2 - core) + slot
            src = x_ref.at[:, o, :]
            dst = recv.at[slot, lax.rem(d, 4), :, d // 4, :]

            def start():
                remote(src, dst, 0, slot, b, to)

            if slot == 0:
                start()
            else:
                pl.when(to_two)(start)
            return c

        def keep():
            local(x_ref.at[:, first + slot, :], recv.at[slot, lax.rem(d, 4), :, d // 4, :], slot)

        if slot == 0:
            keep()
        else:
            pl.when(two)(keep)
        lax.fori_loop(1, 32, send, 0)

    send_orbital(0)
    local(half, half_dst, 2)
    lax.fori_loop(1, 32, send_potential, 0)
    lax.fori_loop(1, 32, greet_again, 0)
    local(w_hbm, w_ref, 12)
    local(c_hbm, c_ref, 13)
    pot[...] = jnp.full(pot.shape, DIAGONAL, F32)

    def unpack(load, store):
        def body(q, c):
            for yb in range(3):
                for j in range(3):
                    rows = to_rows(load(0, yb, q, j), load(1, yb, q, j))
                    for y in range(8):
                        store(yb * 8 + y, pl.ds(pl.multiple_of(q * 24 + 8 * j, 8), 8), rows[y])
            return c

        lax.fori_loop(0, 4, body, 0)

    def chunk(start, t):
        return pl.ds(start + 128 * t, 128)

    def load_potential(side, yb, q, j):
        return [pot_in[side, q, j, :, chunk(yb * 384, t)] for t in range(3)]

    def put(field, y, rows, v):
        field[y, rows, :] = v
        if y < 6 or y >= 18:
            field[24 + y, rows, :] = pltpu.roll(v, 64, 1)

    def store_potential(y, rows, v):
        v = SCALE * v
        pot[y, rows, :] = v + DIAGONAL
        put(field_b, y, rows, field_b[y, rows, :] + (0.5 * v) * field_a[y, rows, :])

    def step(src, dst, weight):
        def block(n):
            y0 = n * ROWS
            values = src[pl.ds(y0, ROWS)].reshape(ROWS * 96, 128)
            high = values.astype(BF16)
            low = (values - high.astype(F32)).astype(BF16)
            along_z = jnp.dot(jnp.concatenate([high, low], 1), w_ref[...], preferred_element_type=F32)
            along_x = []
            for r in range(0, ROWS, 2):
                one, other = slice(96 * r, 96 * r + 96), slice(96 * r + 96, 96 * r + 192)
                columns = jnp.concatenate([jnp.concatenate([high[one], high[other]], 1),
                                           jnp.concatenate([low[one], low[other]], 1)], 0)
                along_x.append(jnp.dot(c_ref[...], columns, preferred_element_type=F32))
            at = [(y0 + s) % 48 for s in range(-6, ROWS + 6)]
            for i in range(12):
                rows = pl.ds(8 * i, 8)
                near = [src[y, rows, :] for y in at]
                for r in range(ROWS):
                    acc = near[6 + r] * pot[y0 + r, rows, :]
                    for k in range(1, 7):
                        acc = acc + COEFS[k] * (near[6 + r + k] + near[6 + r - k])
                    z = along_z[96 * r + 8 * i:96 * r + 8 * i + 8]
                    half_lanes = slice(128 * (r % 2), 128 * (r % 2) + 128)
                    x = (along_x[r // 2][8 * i:8 * i + 8, half_lanes]
                         + along_x[r // 2][96 + 8 * i:96 + 8 * i + 8, half_lanes])
                    acc = acc + ((z[:, :128] + z[:, 128:]) + x)
                    put(dst, y0 + r, rows, weight * acc - dst[y0 + r, rows, :])

        for n in range(24 // ROWS):
            block(n)

    def quarter(band):
        return 14 * band - jnp.maximum(band - 1, 0)

    def spread(slot):
        def share(to_b, to_d):
            begin = 14 * to_b - max(to_b - 1, 0)
            return (pack.at[slot, lax.rem(to_d, 4), pl.ds(begin, TILES), to_d // 4, :],
                    own.at[:, 48 * b + first + slot, :])

        def send(i, c):
            to_d = lax.rem(d + i, 32)
            for to_b in range(4):
                src, dst = share(to_b, to_d)
                remote(src, dst, 2, 3, to_b, to_d)
            return c

        lax.fori_loop(1, 32, send, 0)
        for to_b in range(4):
            src, dst = share(to_b, d)

            @pl.when(to_b == b)
            def _():
                local(src, dst, 3)

            @pl.when(to_b != b)
            def _():
                remote(src, dst, 2, 3, to_b, d)

    def add_potential():
        send_orbital(1)
        arrived(pot_in.at[core], 2)
        remote(pot_in.at[core], pot_in.at[core], 7, 11, partner, d)
        arrived(pot_in.at[core], 11)
        unpack(load_potential, store_potential)

    def filter_orbital(slot, c):
        def load(side, yb, q, j):
            return [recv[slot, q, j, :, chunk(yb * 384 + 1152 * side, t)] for t in range(3)]

        def store(y, rows, v):
            put(field_a, y, rows, v)
            field_b[y, rows, :] = jnp.zeros_like(v)

        def repack(q, c):
            for yb in range(3):
                for j in range(3):
                    rows = [field_a[yb * 8 + y, pl.ds(pl.multiple_of(q * 24 + 8 * j, 8), 8), :] for y in range(8)]
                    left, right = to_tiles(rows)
                    for t in range(3):
                        pack[slot, q, j * 18 + yb * 3 + t] = left[t]
                        pack[slot, q, j * 18 + 9 + yb * 3 + t] = right[t]
            return c

        arrived(recv.at[slot], slot)
        unpack(load, store)

        def steps(t, c):
            step(field_a, field_b, jnp.where(t == 0, 0.5, 1.0))
            pl.when(jnp.logical_and(slot == 0, t == 0))(add_potential)
            step(field_b, field_a, 1.0)
            return c

        lax.fori_loop(0, 2, steps, 0)

        @pl.when(slot == 0)
        def _():
            pl.semaphore_wait(ready, 31)

        lax.fori_loop(0, 4, repack, 0)
        spread(slot)
        return c

    arrived(w_ref, 12)
    arrived(c_ref, 13)
    lax.fori_loop(0, jnp.where(two, 2, 1), filter_orbital, 0)
    arrived(own, 3)

    z_peer = lax.rem(b + 2, 4)
    other = lax.rem(partner + 2, 4)
    PART = EARLY // 2

    def exchange(i):
        tiles = pl.ds(PART * i, PART)
        remote(own.at[tiles], gathered.at[1, tiles], 9, 14 + i, z_peer, d)

    def forward(i):
        tiles = pl.ds(PART * i, PART)
        arrived(gathered.at[1, tiles], 14 + i)
        remote(gathered.at[1, tiles], gathered.at[2, tiles], 11, 17 + i, partner, d)

    total = jnp.zeros((M, M), F32)
    for i in range(0, TILES, 2):
        one = own[i]
        if i == 0:
            one = jnp.where(b >= 2, 0.0, one)
        both = jnp.concatenate([one, own[i + 1]], 1)
        total = total + lax.dot_general(both, both, (((1,), (1,)), ((), ())), precision=lax.Precision.HIGHEST,
                                        preferred_element_type=F32)
    near = total[:, :128]
    far = jnp.concatenate([total[:, 128:], jnp.zeros((M, 64), F32)], 1)
    left_half = lax.broadcasted_iota(jnp.int32, (64, 128), 1) < 64
    packed[0:64] = near[0:64]
    packed[64:128] = jnp.where(left_half, far[0:64], near[64:128])
    packed[128:192] = jnp.where(left_half, far[64:128], pltpu.roll(far[128:192], 64, 1))
    for i in range(8):
        part[i] = packed[24 * i:24 * i + 24]

    mine = zh * 4 + b
    for i in range(1, 8):
        to = lax.rem(mine + i, 8)
        remote(part.at[to], rs_buf.at[mine], 4, 4, lax.rem(to, 4), y_pos * 8 + (to // 4) * 4 + x_pos)
    rs_buf[mine] = part[mine]
    arrived(rs_buf.at[pl.ds(0, 7)], 4)
    exchange(0)
    acc = rs_buf[0]
    for i in range(1, 8):
        acc = acc + rs_buf[i]
    sums[...] = acc
    spot = y_pos * 4 + x_pos
    for i in range(1, 16):
        to = lax.rem(spot + i, 16)
        remote(sums, xy_buf.at[spot], 5, 5, b, (to // 4) * 8 + zh * 4 + lax.rem(to, 4))
    xy_buf[spot] = acc
    arrived(xy_buf.at[pl.ds(0, 15)], 5)
    acc = xy_buf[0]
    for i in range(1, 16):
        acc = acc + xy_buf[i]
    acc = acc / CELLS
    gsum[mine] = acc
    for i in range(1, 8):
        to = lax.rem(mine + i, 8)
        remote(gsum.at[mine], gsum.at[mine], 6, 6, lax.rem(to, 4), y_pos * 8 + (to // 4) * 4 + x_pos)
    arrived(gsum.at[pl.ds(0, 7)], 6)

    exchange(1)
    remote(own.at[pl.ds(0, EARLY)], gathered.at[0, pl.ds(0, EARLY)], 10, 16, partner, d)
    for i in range(8):
        packed[24 * i:24 * i + 24] = gsum[i]
    work[0:64, 0:128] = packed[0:64]
    work[0:64, 128:256] = packed[64:128]
    work[64:128, 0:128] = packed[64:128]
    work[64:128, 128:256] = packed[128:192]
    work[128:192, 0:128] = packed[128:192]
    work[128:192, 128:256] = pltpu.roll(packed[128:192], 64, 1)
    invert_factor(work, inv_ref, wide)

    def place(tile):
        return tile // 18, pl.ds(pl.multiple_of(128 * lax.rem(tile, 18), 128), 128)

    def product(rows, block, n):
        columns = jnp.concatenate([block[2 * n], block[2 * n + 1]], 1)
        return jnp.dot(rows, columns, precision=lax.Precision.HIGHEST, preferred_element_type=F32)

    def rotate(n, c):
        result = product(inv_ref[:, 0:M], own, EARLY // 2 + n)
        for i in range(2):
            plane, lanes = place(quarter(b) + EARLY + 2 * n + i)
            for band in range(4):
                rot[2 * n + i, band] = result[48 * band:48 * band + 48, 128 * i:128 * i + 128]
            for away in (2, 3, 1):
                to = lax.rem(b + away, 4)
                remote(rot.at[2 * n + i, to], out_ref.at[plane, :, lanes], 8, 7 + b, to, d)
            local(rot.at[2 * n + i, b], out_ref.at[plane, :, lanes], 7 + b)
        return c

    def rotate_early(block, band):
        def body(n, c):
            result = product(inv_ref[pl.ds(pl.multiple_of(48 * b, 8), 48), 0:M], block, n)
            for i in range(2):
                plane, lanes = place(quarter(band) + 2 * n + i)

                def keep():
                    out_ref[plane, :, lanes] = result[:, 128 * i:128 * i + 128]

                if i == 0:
                    pl.when(jnp.logical_or(band < 2, n > 0))(keep)
                else:
                    keep()
            return c

        lax.fori_loop(0, EARLY // 2, body, 0)

    lax.fori_loop(0, (TILES - EARLY) // 2, rotate, 0)
    forward(0)
    forward(1)
    rotate_early(own, b)
    arrived(gathered.at[0, pl.ds(0, EARLY)], 16)
    rotate_early(gathered.at[0], partner)
    rotate_early(gathered.at[1], z_peer)
    for i in range(2):
        arrived(gathered.at[2, pl.ds(PART * i, PART)], 17 + i)
    rotate_early(gathered.at[2], other)

    late = TILES - EARLY
    for band in range(4):
        arrived(rot.at[pl.ds(0, late), 0], 7 + band)
    drain(rot.at[0, 0], send_sems.at[8], 3 * late)
    drain(gathered.at[0, pl.ds(0, PART)], send_sems.at[9], 2)
    drain(gathered.at[0, pl.ds(0, EARLY)], send_sems.at[10], 1)
    drain(gathered.at[0, pl.ds(0, PART)], send_sems.at[11], 2)
    orbital = recv.at[0, 0, :, 0, :]
    drain(orbital, send_sems.at[0], jnp.where(two, 46, 47))
    drain(half_dst, send_sems.at[1], 31)
    drain(pot_in.at[0], send_sems.at[7], 1)
    share = pack.at[0, 0, pl.ds(0, TILES), 0, :]
    drain(share, send_sems.at[2], jnp.where(two, 254, 127))
    drain(sums, send_sems.at[4], 7)
    drain(sums, send_sems.at[5], 15)
    drain(sums, send_sems.at[6], 7)


def per_device(orbitals, potential):
    anywhere = pl.BlockSpec(memory_space=pl.ANY)
    out = pl.pallas_call(
        kernel,
        out_shape=jax.ShapeDtypeStruct((3, 48, 2304), F32),
        in_specs=[anywhere] * 4,
        out_specs=pl.BlockSpec(memory_space=pltpu.VMEM),
        scratch_shapes=[
            pltpu.VMEM((2, 4, 3, 8, 2304), F32),
            pltpu.VMEM((2, 4, 3, 8, 1152), F32),
            pltpu.VMEM((256, 256), BF16),
            pltpu.VMEM((192, 192), BF16),
            pltpu.VMEM((48, 96, 128), F32),
            pltpu.VMEM((48, 96, 128), F32),
            pltpu.VMEM((24, 96, 128), F32),
            pltpu.VMEM((2, 4, 54, 8, 128), F32),
            pltpu.VMEM((TILES, M, 128), F32),
            pltpu.VMEM((8, 24, 128), F32),
            pltpu.VMEM((8, 24, 128), F32),
            pltpu.VMEM((16, 24, 128), F32),
            pltpu.VMEM((24, 128), F32),
            pltpu.VMEM((8, 24, 128), F32),
            pltpu.VMEM((M, 128), F32),
            pltpu.VMEM((M, 256), F32),
            pltpu.VMEM((M, 256), F32),
            pltpu.VMEM((128, 128), F32),
            pltpu.VMEM((TILES - EARLY, 4, 48, 128), F32),
            pltpu.VMEM((3, EARLY, M, 128), F32),
            pltpu.SemaphoreType.DMA((12,)),
            pltpu.SemaphoreType.DMA((20,)),
            pltpu.SemaphoreType.REGULAR,
        ],
        compiler_params=pltpu.CompilerParams(
            collective_id=0, has_side_effects=True, vmem_limit_bytes=56 * 2**20),
    )(jnp.transpose(orbitals, (1, 0, 2)), potential, jnp.asarray(z_matrix()), jnp.asarray(x_matrix()))
    return jnp.transpose(out, (1, 0, 2))


def solution(mesh):
    placed = (P("band", "dom", None), P("dom", None))
    return jax.shard_map(
        per_device, mesh=mesh, in_specs=placed, out_specs=P("band", "dom", None), check_vma=False
    )
```
